128 devices in a mesh: ta: 16 (over y, x_lo, core), sa: 8 (over x_hi, z).
Axes of the slice: x: 4 (x_hi: 2, x_lo: 2; x = x_hi * 2 + x_lo), y: 4, z: 4, core: 2. Of those that a mesh axis runs over, the one named last changes fastest.
Arguments:
- propagators: bfloat16 [16, 288, 131072], P('ta', None, 'sa'), may hold values from -6 to 6
- z_sites: int32 [65536], P(('ta', 'sa')), may hold values from 0 to 1023
- z_class: int32 [65536], P(('ta', 'sa')), may hold values from 0 to 31
- kernel_table: float32 [4, 32], replicated, may hold values from -0.00030517578 to 0.00030517578
- pair_combo: int32 [65536, 1], P(('ta', 'sa')), may hold values from 0 to 1023; in each aligned block of 512 rows (0 to 511, 512 to 1023, ...) at most 2 rows name the same one
- pair_site: int32 [65536], P(('ta', 'sa')), may hold values from 0 to 1023
Outputs:
- amplitudes: float32 [2, 65536], P(None, ('ta', 'sa'))
The draws below stay inside these ranges and needn't reach their ends.
Inputs may be any that keep to these rules, and one draw needn't show every extreme that they name: `pair_combo`: in each block of 512 pairs (the pairs of one slab block) no combination is named by more than 2 pairs, a bound that some block reaches.
All inputs are finite; a program needn't handle non-finite values.
Results may differ from the reference program's by a relative error of at most 0.0012.
Values may be sent and summed in bfloat16 or wider, within the bound.
No kernel may reach another device: no remote copies, remote signals or barrier semaphores. Data moves between devices by JAX's collectives and lax.ppermute only.
A program may use at most 192 MiB of HBM per device.

```python
import math
import jax
import jax.numpy as jnp
import numpy as np
from jax import lax

NSC = 12
NSRC = 16
NCLS = 4
NZC = 32
S_DEV = 1024
P_DEV = 512
Z_DEV = 512
NCOMB = 1024
CAP = 2
SITES = 131072
ZTOT = 65536
PTOT = 65536
N_TA = 16
N_SA = 8


def set_ends(entries, own_key, least, top_value):
    spot = [jax.random.randint(jax.random.fold_in(own_key, axis), (), 0, length) for axis, length in enumerate(entries.shape)]
    longest = entries.shape.index(max(entries.shape))
    beside = spot[:longest] + [(spot[longest] + 1) % entries.shape[longest]] + spot[longest + 1:]
    return entries.at[tuple(spot)].set(least).at[tuple(beside)].set(top_value)


def level_of(stream_key, shape, pieces, least, top_value):
    level, own = 1.0, jax.random.fold_in(stream_key, 6)
    for axis_at, shards_of in pieces:
        heights = jnp.exp(jax.random.uniform(jax.random.fold_in(own, axis_at), (shards_of,), jnp.float32, least / len(pieces), top_value / len(pieces)))
        level = level * jnp.repeat(heights, shape[axis_at] // shards_of).reshape([-1 if axis == axis_at else 1 for axis in range(len(shape))])
    return level


def deal_out(stream_key, own, number, rows, count, top, limit, lean):
    sequence = jax.random.permutation(stream_key, count)
    heavy_load, ordinary = load_shares(count, rows * top, limit, lean, True), load_shares(count, rows * top, limit, lean, False)
    places = jnp.arange(count)

    def named(sizes, turn):
        used = int((sizes > 0).sum())
        fixed = max(1, used // 4)
        passed = fixed + (places - fixed + turn * (used - fixed)) % max(1, count - fixed)
        return jnp.zeros((count,), jnp.int32).at[sequence[jnp.where(places < fixed, places, passed)]].set(jnp.asarray(sizes, jnp.int32))

    sizes = jnp.where(number % 4 == 0, named(heavy_load, number // 4), named(ordinary, number - number // 4 - 1))
    mixed = jax.random.permutation(jax.random.fold_in(own, 3), count)
    source_of, receiver = mixed[0:count // 2 * 2:2], mixed[1:count // 2 * 2:2]
    margin = jnp.minimum(sizes[source_of] - 1, limit - sizes[receiver]) // 2
    margin = jnp.where((source_of == sequence[0]) | (receiver == sequence[0]) | (sizes[receiver] == 0), 0, jnp.maximum(margin, 0))
    passed = jax.random.randint(jax.random.fold_in(own, 4), (count // 2,), 0, 1 << 20) % (margin + 1)
    sizes = sizes.at[source_of].add(-passed).at[receiver].add(passed)
    members = jnp.searchsorted(jnp.cumsum(sizes), jnp.arange(rows * top), side="right").astype(jnp.int32)
    grid = members.reshape(top, rows).T
    grid = grid[jax.random.permutation(jax.random.fold_in(own, 1), rows)]
    turn = jax.random.randint(jax.random.fold_in(own, 2), (rows, 1), 0, top)
    return jnp.take_along_axis(grid, (jnp.arange(top)[None, :] + turn) % top, axis=1)


def load_shares(amount, total, most, lean, full):
    portions = [(1 << 20) // math.isqrt(rank ** lean) + 1 for rank in range(1, amount + 1)]
    largest = most if full else min(most, max(-(-total // amount), total * portions[0] // sum(portions)))
    least = 1 if total - largest >= amount - 1 else 0
    counts, spare = [largest] + [least] * (amount - 1), total - largest - least * (amount - 1)
    while spare > 0:
        movable = [i for i in range(1, amount) if counts[i] < largest] or [i for i in range(1, amount) if counts[i] < most]
        whole, budget = sum([portions[i] for i in movable]), spare
        for i in movable:
            more = min(most - counts[i], max(1, budget * portions[i] // whole), spare)
            counts[i] = counts[i] + more
            spare = spare - more
    return np.array(counts)


def normal_values(stream_key, extent, scale, limit, pieces=(), kind=jnp.bfloat16):
    loudness = level_of(stream_key, extent, pieces, -0.22, 0.18) if pieces else 1.0
    array = jax.random.normal(stream_key, extent, jnp.float32) * scale * loudness
    return jnp.minimum(jnp.maximum(array, -limit), limit).astype(kind)


def setup_inputs(seed: int = 0) -> dict:
    seeds = jax.random.split(jax.random.key(seed), 7)
    propagators = normal_values(seeds[0], (NSRC, 2 * NSC * NSC, SITES), 1.0, 6.0, ((0, 16), (2, 8)))
    z_sites = set_ends(jax.random.randint(seeds[1], (ZTOT,), 0, S_DEV), jax.random.fold_in(seeds[1], 1), 0, S_DEV - 1).astype(jnp.int32)
    z_class = set_ends(jax.random.randint(seeds[2], (ZTOT,), 0, NZC), jax.random.fold_in(seeds[2], 1), 0, NZC - 1).astype(jnp.int32)
    kernel_table = normal_values(seeds[3], (NCLS, NZC), (6912 * ZTOT) ** -0.5, 0.00030517578, (), jnp.float32)
    pair_combo_keys = jax.random.split(jax.random.fold_in(seeds[4], 1), PTOT // P_DEV)
    pair_combo_turns = jax.random.permutation(jax.random.fold_in(seeds[4], 3), PTOT // P_DEV)
    pair_combo = jax.vmap(lambda own, number: deal_out(jax.random.fold_in(seeds[4], 2), own, number, P_DEV, NCOMB, 1, CAP, 2))(pair_combo_keys, pair_combo_turns).reshape((PTOT, 1))
    pair_site = set_ends(jax.random.randint(seeds[5], (PTOT,), 0, S_DEV), jax.random.fold_in(seeds[5], 1), 0, S_DEV - 1).astype(jnp.int32)
    return dict(propagators=propagators, z_sites=z_sites, z_class=z_class, kernel_table=kernel_table, pair_combo=pair_combo, pair_site=pair_site)


def global_site(positions, per_block):
    blocks = jnp.arange(positions.shape[0], dtype=jnp.int32) // per_block
    return (blocks % N_SA) * (N_TA * S_DEV) + (blocks // N_SA) * S_DEV + positions.astype(jnp.int32)


def extend_rows(z_rows):
    shaped = z_rows.reshape(z_rows.shape[0], 2, 12, 12, z_rows.shape[-1])
    swapped = jnp.stack([shaped[:, 1], -shaped[:, 0]], axis=1)
    return jnp.stack([shaped, swapped], axis=1)


def trace_pair(combo_mat, prop_mat):
    combo_four = combo_mat.reshape(-1, 2, 12, 12)
    prop_four = jnp.swapaxes(prop_mat.astype(jnp.float32).reshape(-1, 2, 12, 12), 2, 3)
    real_part = jnp.sum(combo_four[:, 0] * prop_four[:, 0] - combo_four[:, 1] * prop_four[:, 1], axis=(1, 2))
    imag_part = jnp.sum(combo_four[:, 0] * prop_four[:, 1] + combo_four[:, 1] * prop_four[:, 0], axis=(1, 2))
    return jnp.stack([real_part, imag_part])


def reference(propagators, z_sites, z_class, kernel_table, pair_combo, pair_site):
    blocks_count = N_TA * N_SA
    z_global = global_site(z_sites, Z_DEV).reshape(blocks_count, Z_DEV)
    classes = z_class.astype(jnp.int32).reshape(blocks_count, Z_DEV)

    def add_block(running, entry):
        indices, class_row = entry
        z_rows = jnp.take(propagators, indices, axis=2)
        weights = kernel_table[:, class_row]
        weighted = (weights[:, None, None, :] * z_rows[None].astype(jnp.float32)).astype(jnp.bfloat16)
        shaped = weighted.reshape(NCLS, NSRC, 2, 12, 12, Z_DEV).astype(jnp.float32)
        extended = extend_rows(z_rows).astype(jnp.float32)
        block_sum = jnp.einsum("cbrliz,asrljz->cabsij", shaped, extended)
        return running + block_sum.reshape(NCOMB, 288), None

    combos, _ = lax.scan(add_block, jnp.zeros((NCOMB, 288), jnp.float32), (z_global, classes))
    combo_ids = pair_combo[:, 0].astype(jnp.int32)
    source_ids = (combo_ids // NSRC) % NSRC
    partner_global = global_site(pair_site, P_DEV)
    partner = propagators[source_ids, :, partner_global]
    return trace_pair(combos[combo_ids], partner)
```

```python
import jax
import jax.numpy as jnp
import numpy as np
from jax import lax
from jax.experimental import pallas as pl
from jax.experimental.pallas import tpu as pltpu
from jax.sharding import PartitionSpec as P

NSC = 12
VMEM = 56 * 1024 * 1024


def one_hot_columns(idx_row, count):
    rows = lax.broadcasted_iota(jnp.int32, (count, idx_row.shape[1]), 0)
    return jnp.where(rows == idx_row, 1.0, 0.0).astype(jnp.bfloat16)


def pick_sites(props, idx, first_row):
    hot = jnp.concatenate(
        [one_hot_columns(idx[r : r + 1, :], props.shape[1]) for r in range(first_row, first_row + 4)],
        axis=1,
    )
    return jnp.dot(props, hot, preferred_element_type=jnp.float32)


def z_gather_kernel(idx_ref, props_ref, out_ref):
    picked = pick_sites(props_ref[0], idx_ref[0], 0)
    count = picked.shape[1]
    half = NSC * NSC
    for l in range(NSC):
        re, im = l * NSC, half + l * NSC
        out_ref[0, :, l * count : (l + 1) * count] = jnp.concatenate(
            [picked[re : re + 8], picked[im : im + 8], picked[re + 8 : re + 12], picked[im + 8 : im + 12]],
            axis=0,
        ).astype(jnp.bfloat16)


def pair_gather_kernel(idx_ref, props_ref, out_ref):
    out_ref[...] = pick_sites(props_ref[0], idx_ref[0], 4).astype(jnp.bfloat16)


def combo_kernel(x_ref, w_ref, out_ref, acc_ref):
    step = pl.program_id(0)
    sources, _, depth = x_ref.shape
    wide = x_ref[...].astype(jnp.float32)
    rows = jnp.concatenate(
        [wide[:, 8 * t : 8 * t + 8, :].reshape(sources * 8, depth) for t in range(3)], axis=0
    )
    right = rows.astype(jnp.bfloat16)
    classes = w_ref.shape[0]
    for c in range(classes):
        left = (rows * w_ref[c : c + 1, :]).astype(jnp.bfloat16)
        part = lax.dot_general(
            right, left, (((1,), (1,)), ((), ())), preferred_element_type=jnp.float32
        )

        @pl.when(step == 0)
        def _():
            acc_ref[c] = part

        @pl.when(step > 0)
        def _():
            acc_ref[c] += part

    @pl.when(step == pl.num_programs(0) - 1)
    def _():
        n = sources * 8
        low_row = lax.broadcasted_iota(jnp.int32, (n, n), 0) % 8 < 4
        low_lane = lax.broadcasted_iota(jnp.int32, (n, n), 1) % 8 < 4

        def swap_rows(m):
            return pltpu.roll(m.reshape(sources, 8, n), 4, 1).reshape(n, n)

        for c in range(classes):
            def blk(i, j):
                return acc_ref[c, n * i : n * i + n, n * j : n * j + n]

            re = blk(0, 0) + blk(1, 1)
            im = blk(1, 0) - blk(0, 1)
            a, b = blk(0, 2), blk(1, 2)
            wide_col = jnp.where(low_lane, a + pltpu.roll(b, n - 4, 1), pltpu.roll(b, 4, 1) - a)
            a, b = blk(2, 0), swap_rows(blk(2, 1))
            tall_row = jnp.where(low_row, a + b, a - b)
            a = blk(2, 2)
            b = swap_rows(pltpu.roll(a, n - 4, 1))
            corner = jnp.where(low_lane, jnp.where(low_row, a + b, a - b), 0.0)
            for k, m in enumerate((re, im, wide_col, tall_row, corner)):
                at = (c * 5 + k) * 8
                out_ref[:, at : at + 8, :] = m.reshape(sources, 8, n)


def spread_matrix():
    out = np.zeros((5, 8, 8, 768), np.float32)

    def put(k, r, q, j, i, imag):
        at = j * NSC + i
        half = NSC * NSC
        if imag:
            out[k, r, q, half + at] = -1.0
            out[k, r, q, 384 + at] = 1.0
        else:
            out[k, r, q, at] = 1.0
            out[k, r, q, 384 + half + at] = 1.0

    for r in range(8):
        for q in range(8):
            put(0, r, q, r, q, False)
            put(1, r, q, r, q, True)
            put(2, r, q, r, 8 + q % 4, q >= 4)
            put(3, r, q, 8 + r % 4, q, r >= 4)
            if q < 4:
                put(4, r, q, 8 + r % 4, 8 + q, r >= 4)
    return out.reshape(320, 768)


def fold_matrix():
    r = np.arange(1024)[:, None] // 128
    q = np.arange(1024)[:, None] % 8
    return (np.arange(64)[None, :] == r * 8 + q).astype(np.float32)


def amplitude_kernel(sums_ref, fold_ref, spread_ref, key_ref, partner_ref, out_ref, q_ref):
    classes, sources = 4, 16

    @pl.when(pl.program_id(0) == 0)
    def _():
        sums = jnp.sum(sums_ref[...], axis=0)
        own = (
            lax.broadcasted_iota(jnp.int32, (sources, 128), 1) // 8
            == lax.broadcasted_iota(jnp.int32, (sources, 128), 0)
        )
        total = jnp.zeros((2 * classes * sources, 768), jnp.float32)
        for k in range(5):
            tall = []
            for c in range(classes):
                at = (c * 5 + k) * 8
                tall.append(
                    jnp.concatenate(
                        [
                            jnp.where(own, jnp.broadcast_to(sums[at + r : at + r + 1, :], (sources, 128)), 0.0)
                            for r in range(8)
                        ],
                        axis=1,
                    )
                )
            tall = jnp.concatenate(tall, axis=0)
            high = tall.astype(jnp.bfloat16)
            low = (tall - high.astype(jnp.float32)).astype(jnp.bfloat16)
            both = jnp.concatenate([high, low], axis=0)
            folded = jnp.dot(both, fold_ref[...], preferred_element_type=jnp.float32)
            total += jnp.dot(
                folded.astype(jnp.bfloat16),
                spread_ref[64 * k : 64 * k + 64, :],
                preferred_element_type=jnp.float32,
            )
        q_ref[0:128, :] = total[:, 0:288].astype(jnp.bfloat16)
        q_ref[128:256, :] = total[:, 384:672].astype(jnp.bfloat16)

    traces = jnp.dot(q_ref[...], partner_ref[...], preferred_element_type=jnp.float32)
    combos = classes * sources
    here = lax.broadcasted_iota(jnp.int32, (combos, 128), 0)
    blocks, _, count = key_ref.shape
    for u in range(blocks):
        for g in range(count // 128):
            lanes = slice(u * count + g * 128, u * count + g * 128 + 128)
            mask = here == key_ref[u, :, g * 128 : g * 128 + 128]
            for part in range(2):
                at = part * 2 * combos
                value = traces[at : at + combos, lanes] + traces[at + combos : at + 2 * combos, lanes]
                out_ref[u, part : part + 1, g * 128 : g * 128 + 128] = jnp.sum(
                    jnp.where(mask, value, 0.0), axis=0, keepdims=True
                )


def params():
    return pltpu.CompilerParams(vmem_limit_bytes=VMEM)


def local(propagators, z_sites, z_class, kernel_table, pair_combo, pair_site):
    slabs = lax.axis_size("ta")
    blocks = lax.axis_size("sa")
    me = lax.axis_index("ta")
    rows = propagators.shape[1]
    site_count = propagators.shape[2] // slabs
    z_count = z_sites.shape[0]
    pair_count = pair_site.shape[0]
    classes = kernel_table.shape[0]
    depth = NSC * z_count

    def exchange(array, axis):
        return lax.all_to_all(array, axis, split_axis=0, concat_axis=0, tiled=True)

    lists = jnp.concatenate([z_sites, pair_site, pair_combo[:, 0]]).reshape(1, -1, 128)
    lists = exchange(jnp.broadcast_to(lists, (slabs,) + lists.shape[1:]), "ta")

    idx_spec = pl.BlockSpec((1,) + lists.shape[1:], lambda t: (t, 0, 0))
    props_spec = pl.BlockSpec((1, rows, site_count), lambda t: (0, 0, t))
    z_rows = pl.pallas_call(
        z_gather_kernel,
        grid=(slabs,),
        in_specs=[idx_spec, props_spec],
        out_specs=pl.BlockSpec((1, 24, depth), lambda t: (t, 0, 0)),
        out_shape=jax.ShapeDtypeStruct((slabs, 24, depth), jnp.bfloat16),
        compiler_params=params(),
        cost_estimate=pl.CostEstimate(
            flops=2 * rows * site_count * z_count * slabs, bytes_accessed=15_000_000, transcendentals=0
        ),
        name="z_gather",
    )(lists, propagators)
    z_rows = exchange(z_rows, "ta")

    partner = pl.pallas_call(
        pair_gather_kernel,
        grid=(slabs,),
        in_specs=[idx_spec, props_spec],
        out_specs=pl.BlockSpec((rows, pair_count), lambda t: (0, t)),
        out_shape=jax.ShapeDtypeStruct((rows, slabs * pair_count), jnp.bfloat16),
        compiler_params=params(),
        cost_estimate=pl.CostEstimate(
            flops=2 * rows * site_count * pair_count * slabs, bytes_accessed=15_000_000, transcendentals=0
        ),
        name="pair_gather",
    )(lists, propagators)
    combo_ids = lists[:, 8:12, :].reshape(slabs, 1, pair_count)
    key = jnp.where(combo_ids // 16 % 16 == me, combo_ids // 256 * 16 + combo_ids % 16, -1)

    one_hot = (
        z_class[None, :] == jnp.arange(kernel_table.shape[1], dtype=jnp.int32)[:, None]
    ).astype(jnp.float32)
    weights = jnp.dot(kernel_table, one_hot, precision=lax.Precision.HIGHEST)

    per_step = 2
    sums = pl.pallas_call(
        combo_kernel,
        grid=(NSC // per_step,),
        in_specs=[
            pl.BlockSpec((slabs, 24, per_step * z_count), lambda l: (0, 0, l)),
            pl.BlockSpec((classes, per_step * z_count), lambda l: (0, 0)),
        ],
        out_specs=pl.BlockSpec((slabs, classes * 40, 128), lambda l: (0, 0, 0)),
        out_shape=jax.ShapeDtypeStruct((slabs, classes * 40, 128), jnp.float32),
        scratch_shapes=[pltpu.VMEM((classes, slabs * 24, slabs * 24), jnp.float32)],
        compiler_params=params(),
        cost_estimate=pl.CostEstimate(
            flops=2 * classes * 384 * 384 * depth, bytes_accessed=6_000_000, transcendentals=0
        ),
        name="combo_sums",
    )(z_rows, jnp.tile(weights, (1, per_step)))

    sums = jnp.sum(exchange(sums, "ta"), axis=0)
    sums = exchange(jnp.broadcast_to(sums[None], (blocks,) + sums.shape), "sa")

    group = 2
    found = pl.pallas_call(
        amplitude_kernel,
        grid=(slabs // group,),
        in_specs=[
            pl.BlockSpec(sums.shape, lambda t: (0, 0, 0)),
            pl.BlockSpec((1024, 64), lambda t: (0, 0)),
            pl.BlockSpec((320, 768), lambda t: (0, 0)),
            pl.BlockSpec((group, 1, pair_count), lambda t: (t, 0, 0)),
            pl.BlockSpec((rows, group * pair_count), lambda t: (0, t)),
        ],
        out_specs=pl.BlockSpec((group, 2, pair_count), lambda t: (t, 0, 0)),
        out_shape=jax.ShapeDtypeStruct((slabs, 2, pair_count), jnp.float32),
        scratch_shapes=[pltpu.VMEM((256, 288), jnp.bfloat16)],
        compiler_params=params(),
        name="amplitudes",
    )(
        sums,
        jnp.asarray(fold_matrix(), jnp.bfloat16),
        jnp.asarray(spread_matrix(), jnp.bfloat16),
        key,
        partner,
    )
    return jnp.sum(exchange(found, "ta"), axis=0)


def solution(mesh):
    placed = (
        P("ta", None, "sa"),
        P(("ta", "sa")),
        P(("ta", "sa")),
        P(),
        P(("ta", "sa"), None),
        P(("ta", "sa")),
    )
    return jax.shard_map(
        local, mesh=mesh, in_specs=placed, out_specs=P(None, ("ta", "sa")), check_vma=False
    )
```

```python
import functools

import jax
import jax.numpy as jnp
import numpy as np
from jax import lax
from jax.experimental import pallas as pl
from jax.experimental.pallas import tpu as pltpu
from jax.sharding import PartitionSpec as P

NSC = 12

def one_hot_columns(idx_row, count):
    rows = lax.broadcasted_iota(jnp.int32, (count, idx_row.shape[1]), 0)
    return jnp.where(rows == idx_row, 1.0, 0.0).astype(jnp.bfloat16)


def z_gather_kernel(idx_ref, props_ref, after_ref, out_ref, held_ref, sems):
    slabs = out_ref.shape[0]
    count = out_ref.shape[2] // NSC

    def send(t):
        return pltpu.make_async_copy(held_ref.at[t], out_ref.at[t], sems.at[t])

    sites = props_ref.shape[2] // slabs
    half = NSC * NSC

    def pair_of_slabs(u, carry):
        for t in (2 * u, 2 * u + 1):
            idx = idx_ref[t]
            hot = jnp.concatenate([one_hot_columns(idx[r : r + 1, :], sites) for r in range(4)], axis=1)
            block = props_ref[0, :, pl.ds(pl.multiple_of(t * sites, sites), sites)]
            picked = jnp.dot(block, hot, preferred_element_type=jnp.float32)
            for l in range(NSC):
                re, im = l * NSC, half + l * NSC
                held_ref[t, :, l * count : (l + 1) * count] = jnp.concatenate(
                    [
                        picked[re : re + 8],
                        picked[im : im + 8],
                        picked[re + 8 : re + 12],
                        picked[im + 8 : im + 12],
                    ],
                    axis=0,
                ).astype(jnp.bfloat16)
            send(t).start()
        return carry

    lax.fori_loop(0, slabs // 2, pair_of_slabs, 0)
    for t in range(slabs):
        send(t).wait()


def pair_pick_kernel(me_ref, idx_ref, props_ref, out_ref):
    slabs = idx_ref.shape[0]
    sites = props_ref.shape[2] // slabs
    lax.fori_loop(0, slabs, functools.partial(pick_block, me_ref, idx_ref, props_ref, out_ref, sites), 0)


def pick_block(me_ref, idx_ref, props_ref, out_ref, sites, t, carry):
    idx = idx_ref[t]
    far = 1 << 20
    ids = lax.broadcasted_iota(jnp.int32, (64, 128), 0)
    lane = lax.broadcasted_iota(jnp.int32, (1, 128), 1)
    first = jnp.full((64, 128), far, jnp.int32)
    last = jnp.full((64, 128), -1, jnp.int32)
    for r in range(4):
        combo = idx[8 + r : 9 + r, :]
        key = jnp.where(combo // 16 % 16 == me_ref[0], combo // 256 * 16 + combo % 16, -1)
        code = (r * 128 + lane) * sites + idx[4 + r : 5 + r, :]
        mine = ids == key
        first = jnp.minimum(first, jnp.where(mine, code, far))
        last = jnp.maximum(last, jnp.where(mine, code, -1))
    first = jnp.min(first, axis=1, keepdims=True)
    last = jnp.max(last, axis=1, keepdims=True)
    found = jnp.concatenate([first, last], axis=0)
    place = jnp.where((found >= 0) & (found < far), found % sites, -1)
    hot = jnp.where(
        lax.broadcasted_iota(jnp.int32, (128, sites), 1) == place, 1.0, 0.0
    ).astype(jnp.bfloat16)
    block = props_ref[0, :, pl.ds(pl.multiple_of(t * sites, sites), sites)]
    out_ref[:, pl.ds(pl.multiple_of(t * 128, 128), 128)] = lax.dot_general(
        block, hot, (((1,), (1,)), ((), ())), preferred_element_type=jnp.float32
    ).astype(jnp.bfloat16)
    return carry


def combo_kernel(x_ref, w_ref, after_ref, out_ref, held_ref, acc_ref, sems):
    sources, _, lanes = x_ref.shape
    classes, count = w_ref.shape
    per = 4
    depth = per * count
    n = sources * 8

    def piece(s):
        at = pl.ds(pl.multiple_of(s * depth, depth), depth)
        return pltpu.make_async_copy(x_ref.at[:, :, at], held_ref.at[s], sems.at[s])

    for s in range(lanes // depth):
        piece(s).start()

    def chunk(s, carry):
        piece(s).wait()
        wide = held_ref[s].astype(jnp.float32)
        rows = jnp.concatenate(
            [wide[:, 8 * t : 8 * t + 8, :].reshape(n, depth) for t in range(3)], axis=0
        )
        right = rows.astype(jnp.bfloat16)
        left = jnp.concatenate(
            [
                (rows * jnp.concatenate([w_ref[c : c + 1, :]] * per, axis=1)).astype(jnp.bfloat16)
                for c in range(classes)
            ],
            axis=0,
        )
        part = lax.dot_general(
            left, right, (((1,), (1,)), ((), ())), preferred_element_type=jnp.float32
        )

        @pl.when(s == 0)
        def _():
            acc_ref[...] = part

        @pl.when(s > 0)
        def _():
            acc_ref[...] += part

        return carry

    lax.fori_loop(0, lanes // depth, chunk, 0)

    low_row = lax.broadcasted_iota(jnp.int32, (n, n), 0) % 8 < 4
    low_lane = lax.broadcasted_iota(jnp.int32, (n, n), 1) % 8 < 4

    def swap_rows(m):
        return pltpu.roll(m.reshape(sources, 8, n), 4, 1).reshape(n, n)

    def swap_lanes(m):
        return jnp.where(low_lane, pltpu.roll(m, n - 4, 1), pltpu.roll(m, 4, 1))

    for c in range(classes):

        def blk(a_tile, b_tile):
            at = c * 3 * n + n * b_tile
            return acc_ref[at : at + n, n * a_tile : n * a_tile + n]

        re = blk(0, 0) + blk(1, 1)
        im = blk(1, 0) - blk(0, 1)
        a, b = blk(0, 2), swap_rows(blk(1, 2))
        wide_col = jnp.where(low_row, a + b, b - a)
        a, b = blk(2, 0), swap_lanes(blk(2, 1))
        tall_row = jnp.where(low_lane, a + b, a - b)
        a = blk(2, 2)
        b = swap_lanes(swap_rows(a))
        corner = jnp.where(low_row, jnp.where(low_lane, a + b, a - b), 0.0)
        for k, m in enumerate((re, im, wide_col, tall_row, corner)):
            at = (c * 5 + k) * 8
            out_ref[:, at : at + 8, :] = m.T.reshape(sources, 8, n)


def spread_matrix():
    out = np.zeros((5, 8, 8, 768), np.float32)

    def put(k, r, q, j, i, imag):
        at = j * NSC + i
        half = NSC * NSC
        if imag:
            out[k, r, q, half + at] = -1.0
            out[k, r, q, 384 + at] = 1.0
        else:
            out[k, r, q, at] = 1.0
            out[k, r, q, 384 + half + at] = 1.0

    for r in range(8):
        for q in range(8):
            put(0, r, q, r, q, False)
            put(1, r, q, r, q, True)
            put(2, r, q, r, 8 + q % 4, q >= 4)
            put(3, r, q, 8 + r % 4, q, r >= 4)
            if q < 4:
                put(4, r, q, 8 + r % 4, 8 + q, r >= 4)
    return out.reshape(320, 768)


def fold_matrix():
    r = np.arange(1024)[:, None] // 128
    q = np.arange(1024)[:, None] % 8
    return (np.arange(64)[None, :] == r * 8 + q).astype(np.float32)


def amplitude_kernel(sums_ref, fold_ref, spread_ref, partner_ref, out_ref):
    classes, sources = 4, 16
    combos = classes * sources
    sums = jnp.sum(sums_ref[...], axis=0)
    own = (
        lax.broadcasted_iota(jnp.int32, (sources, 128), 1) // 8
        == lax.broadcasted_iota(jnp.int32, (sources, 128), 0)
    )
    total = jnp.zeros((2 * combos, 768), jnp.float32)
    for k in range(5):
        tall = []
        for c in range(classes):
            at = (c * 5 + k) * 8
            tall.append(
                jnp.concatenate(
                    [
                        jnp.where(own, jnp.broadcast_to(sums[at + r : at + r + 1, :], (sources, 128)), 0.0)
                        for r in range(8)
                    ],
                    axis=1,
                )
            )
        tall = jnp.concatenate(tall, axis=0)
        high = tall.astype(jnp.bfloat16)
        low = (tall - high.astype(jnp.float32)).astype(jnp.bfloat16)
        both = jnp.concatenate([high, low], axis=0)
        folded = jnp.dot(both, fold_ref[...], preferred_element_type=jnp.float32)
        total += jnp.dot(
            folded.astype(jnp.bfloat16),
            spread_ref[64 * k : 64 * k + 64, :],
            preferred_element_type=jnp.float32,
        )
    rows = partner_ref.shape[0]
    probe = jnp.concatenate([total[:, 0:rows], total[:, 384 : 384 + rows]], axis=0).astype(jnp.bfloat16)
    traces = jnp.dot(probe, partner_ref[...], preferred_element_type=jnp.float32)
    mine = (
        lax.broadcasted_iota(jnp.int32, (combos, 128), 1) % combos
        == lax.broadcasted_iota(jnp.int32, (combos, 128), 0)
    )
    for t in range(out_ref.shape[0]):
        lanes = slice(t * 128, t * 128 + 128)
        for part in range(2):
            at = part * 2 * combos
            value = traces[at : at + combos, lanes] + traces[at + combos : at + 2 * combos, lanes]
            out_ref[t, part : part + 1, :] = jnp.sum(jnp.where(mine, value, 0.0), axis=0, keepdims=True)


def home_kernel(back_ref, slot_ref, source_ref, out_ref):
    sources, _, slots = back_ref.shape
    pairs = slot_ref.shape[1]
    rest = jnp.concatenate([back_ref[:, 0, :], back_ref[:, 1, :]], axis=0)
    parts = []
    for _ in range(3):
        part = rest.astype(jnp.bfloat16)
        rest = rest - part.astype(jnp.float32)
        parts.append(part)
    hot = jnp.where(
        lax.broadcasted_iota(jnp.int32, (slots, pairs), 0) == slot_ref[...], 1.0, 0.0
    ).astype(jnp.bfloat16)
    spread = jnp.dot(jnp.concatenate(parts, axis=0), hot, preferred_element_type=jnp.float32)
    n = 2 * sources
    value = (spread[0:n] + spread[n : 2 * n]) + spread[2 * n : 3 * n]
    mine = lax.broadcasted_iota(jnp.int32, (sources, pairs), 0) == source_ref[...]
    for part in range(2):
        out_ref[part : part + 1, :] = jnp.sum(
            jnp.where(mine, value[part * sources : (part + 1) * sources], 0.0), axis=0, keepdims=True
        )


def params(mebibytes):
    return pltpu.CompilerParams(vmem_limit_bytes=mebibytes * 1024 * 1024)


IN_VMEM = pl.BlockSpec(memory_space=pltpu.VMEM)


def local(propagators, z_sites, z_class, kernel_table, pair_combo, pair_site):
    slabs = lax.axis_size("ta")
    blocks = lax.axis_size("sa")
    me = lax.axis_index("ta")
    rows = propagators.shape[1]
    site_count = propagators.shape[2] // slabs
    z_count = z_sites.shape[0]
    pair_count = pair_site.shape[0]
    classes = kernel_table.shape[0]
    depth = NSC * z_count

    def exchange(array, axis):
        return lax.all_to_all(array, axis, split_axis=0, concat_axis=0, tiled=True)

    lists = jnp.concatenate([z_sites, pair_site, pair_combo[:, 0]]).reshape(1, -1, 128)
    lists = exchange(jnp.broadcast_to(lists, (slabs,) + lists.shape[1:]), "ta")

    one_hot = (
        z_class[None, :] == jnp.arange(kernel_table.shape[1], dtype=jnp.int32)[:, None]
    ).astype(jnp.float32)
    weights = jnp.dot(kernel_table, one_hot, precision=lax.Precision.HIGHEST)

    z_rows = pl.pallas_call(
        z_gather_kernel,
        in_specs=[IN_VMEM, IN_VMEM, pl.BlockSpec(memory_space=pl.ANY)],
        out_specs=pl.BlockSpec(memory_space=pl.ANY),
        out_shape=jax.ShapeDtypeStruct((slabs, 24, depth), jnp.bfloat16),
        scratch_shapes=[
            pltpu.VMEM((slabs, 24, depth), jnp.bfloat16),
            pltpu.SemaphoreType.DMA((slabs,)),
        ],
        compiler_params=params(52),
        cost_estimate=pl.CostEstimate(
            flops=2 * rows * site_count * z_count * slabs, bytes_accessed=15_000_000, transcendentals=0
        ),
        name="z_gather",
    )(lists, propagators, weights)
    z_rows = exchange(z_rows, "ta")

    slots = 128
    partner = pl.pallas_call(
        pair_pick_kernel,
        in_specs=[pl.BlockSpec(memory_space=pltpu.SMEM), IN_VMEM, IN_VMEM],
        out_specs=IN_VMEM,
        out_shape=jax.ShapeDtypeStruct((rows, slabs * slots), jnp.bfloat16),
        compiler_params=params(16),
        cost_estimate=pl.CostEstimate(
            flops=2 * rows * site_count * slots * slabs, bytes_accessed=11_000_000, transcendentals=0
        ),
        name="pair_pick",
    )(me.astype(jnp.int32).reshape(1), lists, propagators)

    combo_ids = pair_combo[:, 0]
    counter = jnp.arange(pair_count, dtype=jnp.int32)
    second = jnp.any(
        (combo_ids[:, None] == combo_ids[None, :]) & (counter[None, :] < counter[:, None]), axis=1
    )
    slot = combo_ids // 256 * 16 + combo_ids % 16 + jnp.where(second, 64, 0)
    source = combo_ids // 16 % 16

    sums = pl.pallas_call(
        combo_kernel,
        in_specs=[pl.BlockSpec(memory_space=pl.ANY), IN_VMEM, pl.BlockSpec(memory_space=pl.ANY)],
        out_specs=IN_VMEM,
        out_shape=jax.ShapeDtypeStruct((slabs, classes * 40, 128), jnp.float32),
        scratch_shapes=[
            pltpu.VMEM((3, slabs, 24, depth // 3), jnp.bfloat16),
            pltpu.VMEM((classes * slabs * 24, slabs * 24), jnp.float32),
            pltpu.SemaphoreType.DMA((3,)),
        ],
        compiler_params=params(32),
        cost_estimate=pl.CostEstimate(
            flops=2 * classes * 384 * 384 * depth, bytes_accessed=6_000_000, transcendentals=0
        ),
        name="combo_sums",
    )(z_rows, weights, partner)

    sums = jnp.sum(exchange(sums, "ta"), axis=0)
    sums = exchange(jnp.broadcast_to(sums[None], (blocks,) + sums.shape), "sa")

    found = pl.pallas_call(
        amplitude_kernel,
        in_specs=[IN_VMEM] * 4,
        out_specs=IN_VMEM,
        out_shape=jax.ShapeDtypeStruct((slabs, 2, slots), jnp.float32),
        compiler_params=params(32),
        name="amplitudes",
    )(
        sums,
        jnp.asarray(fold_matrix(), jnp.bfloat16),
        jnp.asarray(spread_matrix(), jnp.bfloat16),
        partner,
    )
    back = exchange(found, "ta")
    return pl.pallas_call(
        home_kernel,
        in_specs=[IN_VMEM] * 3,
        out_specs=IN_VMEM,
        out_shape=jax.ShapeDtypeStruct((2, pair_count), jnp.float32),
        compiler_params=params(16),
        name="home",
    )(back, slot.reshape(1, -1), source.reshape(1, -1))


def solution(mesh):
    placed = (
        P("ta", None, "sa"),
        P(("ta", "sa")),
        P(("ta", "sa")),
        P(),
        P(("ta", "sa"), None),
        P(("ta", "sa")),
    )
    return jax.shard_map(
        local, mesh=mesh, in_specs=placed, out_specs=P(None, ("ta", "sa")), check_vma=False
    )
```

```python
import functools

import jax
import jax.numpy as jnp
import numpy as np
from jax import lax
from jax.experimental import pallas as pl
from jax.experimental.pallas import tpu as pltpu
from jax.sharding import PartitionSpec as P

NSC = 12

def one_hot_columns(idx_row, count):
    rows = lax.broadcasted_iota(jnp.int32, (count, idx_row.shape[1]), 0)
    return jnp.where(rows == idx_row, 1.0, 0.0).astype(jnp.bfloat16)


def z_gather_kernel(idx_ref, props_ref, after_ref, out_ref, block_ref, held_ref, in_sems, out_sems):
    slabs = out_ref.shape[0]
    count = out_ref.shape[2] // NSC
    steps = block_ref.shape[0]
    per = slabs // steps
    lanes = block_ref.shape[2]
    sites = lanes // per
    half = NSC * NSC
    ahead = 3

    def fetch(u):
        at = pl.ds(pl.multiple_of(u * lanes, lanes), lanes)
        return pltpu.make_async_copy(props_ref.at[0, :, at], block_ref.at[u], in_sems.at[u])

    def send(u):
        at = pl.ds(u * per, per)
        return pltpu.make_async_copy(held_ref.at[at], out_ref.at[at], out_sems.at[u])

    for u in range(ahead):
        fetch(u).start()

    def step(u, carry):
        fetch(u).wait()

        @pl.when(u + ahead < steps)
        def _():
            fetch(u + ahead).start()

        for k in range(per):
            t = u * per + k
            idx = idx_ref[t]
            hot = jnp.concatenate([one_hot_columns(idx[r : r + 1, :], sites) for r in range(4)], axis=1)
            block = block_ref[u, :, k * sites : (k + 1) * sites]
            picked = jnp.dot(block, hot, preferred_element_type=jnp.float32)
            for l in range(NSC):
                re, im = l * NSC, half + l * NSC
                held_ref[t, :, l * count : (l + 1) * count] = jnp.concatenate(
                    [
                        picked[re : re + 8],
                        picked[im : im + 8],
                        picked[re + 8 : re + 12],
                        picked[im + 8 : im + 12],
                    ],
                    axis=0,
                ).astype(jnp.bfloat16)
        send(u).start()
        return carry

    lax.fori_loop(0, steps, step, 0)
    for u in range(steps):
        send(u).wait()


def pair_pick_kernel(me_ref, idx_ref, props_ref, out_ref):
    slabs = idx_ref.shape[0]
    sites = props_ref.shape[2] // slabs
    lax.fori_loop(0, slabs, functools.partial(pick_block, me_ref, idx_ref, props_ref, out_ref, sites), 0)


def pick_block(me_ref, idx_ref, props_ref, out_ref, sites, t, carry):
    idx = idx_ref[t]
    far = 1 << 20
    ids = lax.broadcasted_iota(jnp.int32, (64, 128), 0)
    lane = lax.broadcasted_iota(jnp.int32, (1, 128), 1)
    first = jnp.full((64, 128), far, jnp.int32)
    last = jnp.full((64, 128), -1, jnp.int32)
    for r in range(4):
        combo = idx[8 + r : 9 + r, :]
        key = jnp.where(combo // 16 % 16 == me_ref[0], combo // 256 * 16 + combo % 16, -1)
        code = (r * 128 + lane) * sites + idx[4 + r : 5 + r, :]
        mine = ids == key
        first = jnp.minimum(first, jnp.where(mine, code, far))
        last = jnp.maximum(last, jnp.where(mine, code, -1))
    first = jnp.min(first, axis=1, keepdims=True)
    last = jnp.max(last, axis=1, keepdims=True)
    found = jnp.concatenate([first, last], axis=0)
    place = jnp.where((found >= 0) & (found < far), found % sites, -1)
    hot = jnp.where(
        lax.broadcasted_iota(jnp.int32, (128, sites), 1) == place, 1.0, 0.0
    ).astype(jnp.bfloat16)
    block = props_ref[0, :, pl.ds(pl.multiple_of(t * sites, sites), sites)]
    out_ref[:, pl.ds(pl.multiple_of(t * 128, 128), 128)] = lax.dot_general(
        block, hot, (((1,), (1,)), ((), ())), preferred_element_type=jnp.float32
    ).astype(jnp.bfloat16)
    return carry


def coded(sums):
    groups, rows, lanes = sums.shape
    lane = lax.broadcasted_iota(jnp.int32, (groups, lanes), 1)
    tail_row = lax.broadcasted_iota(jnp.int32, (groups, 16, lanes), 1)
    tail = jnp.zeros((groups, 16, lanes), jnp.int32)
    whole = []
    for c in range(rows // 40):
        part = sums[:, 40 * c : 40 * c + 40, :]
        peak = jnp.max(jnp.abs(part), axis=1)
        for d in (4, 2, 1):
            other = jnp.where(
                lane % (2 * d) < d, pltpu.roll(peak, lanes - d, 1), pltpu.roll(peak, d, 1)
            )
            peak = jnp.maximum(peak, other)
        shift = 14.0 - jnp.floor(jnp.log2(jnp.maximum(peak, 2.0**-112)))
        value = jnp.floor(part * jnp.exp2(shift)[:, None, :] + 0.5)
        whole.append(jnp.clip(value, -32767.0, 32767.0).astype(jnp.int32))
        tail = jnp.where(tail_row == c, shift.astype(jnp.int32)[:, None, :], tail)
    return jnp.concatenate(whole + [tail], axis=1).astype(jnp.int16)


def decoded_sum(coded_ref):
    total = None
    for g in range(coded_ref.shape[0]):
        value = coded_ref[g].astype(jnp.int32).astype(jnp.float32)
        rows = value.shape[0] - 16
        parts = []
        for c in range(rows // 40):
            scale = jnp.exp2(-value[rows + c : rows + c + 1, :])
            parts.append(value[40 * c : 40 * c + 40, :] * scale)
        term = jnp.concatenate(parts, axis=0)
        total = term if total is None else total + term
    return total


def combo_kernel(x_ref, w_ref, after_a, after_b, after_c, out_ref, held_ref, acc_ref, last_ref, sums_ref, sems):
    sources, _, lanes = x_ref.shape
    classes, count = w_ref.shape
    per = 4
    depth = per * count
    n = sources * 8

    def piece(s):
        at = pl.ds(pl.multiple_of(s * depth, depth), depth)
        return pltpu.make_async_copy(x_ref.at[:, :, at], held_ref.at[s], sems.at[s])

    for s in range(lanes // depth):
        piece(s).start()

    def chunk(s, carry):
        piece(s).wait()
        wide = held_ref[s].astype(jnp.float32)
        rows = jnp.concatenate(
            [wide[:, 8 * t : 8 * t + 8, :].reshape(n, depth) for t in range(3)], axis=0
        )
        right = rows.astype(jnp.bfloat16)
        scaled = [
            rows * jnp.concatenate([w_ref[c : c + 1, :]] * per, axis=1) for c in range(classes)
        ]
        left = jnp.concatenate(
            [scaled[c][n * t : n * t + n, :] for t in range(3) for c in range(classes)], axis=0
        ).astype(jnp.bfloat16)
        contract = (((1,), (1,)), ((), ()))
        main = lax.dot_general(left, right[0 : 2 * n], contract, preferred_element_type=jnp.float32)
        last = lax.dot_general(
            left[2 * classes * n :], right[2 * n :], contract, preferred_element_type=jnp.float32
        )

        @pl.when(s == 0)
        def _():
            acc_ref[...] = main
            last_ref[...] = last

        @pl.when(s > 0)
        def _():
            acc_ref[...] += main
            last_ref[...] += last

        return carry

    lax.fori_loop(0, lanes // depth, chunk, 0)

    low_row = lax.broadcasted_iota(jnp.int32, (n, n), 0) % 8 < 4
    low_lane = lax.broadcasted_iota(jnp.int32, (n, n), 1) % 8 < 4

    def swap_rows(m):
        return pltpu.roll(m.reshape(sources, 8, n), 4, 1).reshape(n, n)

    def swap_lanes(m):
        return jnp.where(low_lane, pltpu.roll(m, n - 4, 1), pltpu.roll(m, 4, 1))

    for c in range(classes):

        def blk(left_tile, right_tile):
            at = (left_tile * classes + c) * n
            return acc_ref[at : at + n, n * right_tile : n * right_tile + n]

        re = (blk(0, 0) + blk(1, 1)).T
        im = (blk(0, 1) - blk(1, 0)).T
        a, b = blk(2, 0), swap_rows(blk(2, 1))
        wide_col = jnp.where(low_row, a + b, b - a).T
        tall_row = jnp.where(low_row, a + b, a - b)
        a = last_ref[c * n : c * n + n, :]
        b = swap_lanes(swap_rows(a))
        corner = jnp.where(low_row, jnp.where(low_lane, a + b, a - b), 0.0).T
        for k, m in enumerate((re, im, wide_col, tall_row, corner)):
            at = (c * 5 + k) * 8
            sums_ref[:, at : at + 8, :] = m.reshape(sources, 8, n)
    out_ref[...] = coded(sums_ref[...])


def reduce_kernel(coded_ref, out_ref):
    total = coded(decoded_sum(coded_ref)[None])
    for g in range(out_ref.shape[0]):
        out_ref[g] = total[0]


def spread_matrix():
    out = np.zeros((5, 8, 8, 768), np.float32)

    def put(k, r, q, j, i, imag):
        at = j * NSC + i
        half = NSC * NSC
        if imag:
            out[k, r, q, half + at] = -1.0
            out[k, r, q, 384 + at] = 1.0
        else:
            out[k, r, q, at] = 1.0
            out[k, r, q, 384 + half + at] = 1.0

    for r in range(8):
        for q in range(8):
            put(0, r, q, r, q, False)
            put(1, r, q, r, q, True)
            put(2, r, q, r, 8 + q % 4, q >= 4)
            put(3, r, q, 8 + r % 4, q, r >= 4)
            if q < 4:
                put(4, r, q, 8 + r % 4, 8 + q, r >= 4)
    return out.reshape(320, 768)


def fold_matrix():
    r = np.arange(1024)[:, None] // 128
    q = np.arange(1024)[:, None] % 8
    return (np.arange(64)[None, :] == r * 8 + q).astype(np.float32)


def amplitude_kernel(sums_ref, fold_ref, spread_ref, partner_ref, out_ref):
    classes, sources = 4, 16
    combos = classes * sources
    sums = decoded_sum(sums_ref)
    own = (
        lax.broadcasted_iota(jnp.int32, (sources, 128), 1) // 8
        == lax.broadcasted_iota(jnp.int32, (sources, 128), 0)
    )
    total = jnp.zeros((2 * combos, 768), jnp.float32)
    for k in range(5):
        tall = []
        for c in range(classes):
            at = (c * 5 + k) * 8
            tall.append(
                jnp.concatenate(
                    [
                        jnp.where(own, jnp.broadcast_to(sums[at + r : at + r + 1, :], (sources, 128)), 0.0)
                        for r in range(8)
                    ],
                    axis=1,
                )
            )
        tall = jnp.concatenate(tall, axis=0)
        high = tall.astype(jnp.bfloat16)
        low = (tall - high.astype(jnp.float32)).astype(jnp.bfloat16)
        both = jnp.concatenate([high, low], axis=0)
        folded = jnp.dot(both, fold_ref[...], preferred_element_type=jnp.float32)
        total += jnp.dot(
            folded.astype(jnp.bfloat16),
            spread_ref[64 * k : 64 * k + 64, :],
            preferred_element_type=jnp.float32,
        )
    rows = partner_ref.shape[0]
    probe = jnp.concatenate([total[:, 0:rows], total[:, 384 : 384 + rows]], axis=0).astype(jnp.bfloat16)
    traces = jnp.dot(probe, partner_ref[...], preferred_element_type=jnp.float32)
    mine = (
        lax.broadcasted_iota(jnp.int32, (combos, 128), 1) % combos
        == lax.broadcasted_iota(jnp.int32, (combos, 128), 0)
    )
    for t in range(out_ref.shape[0]):
        lanes = slice(t * 128, t * 128 + 128)
        for part in range(2):
            at = part * 2 * combos
            value = traces[at : at + combos, lanes] + traces[at + combos : at + 2 * combos, lanes]
            out_ref[t, part : part + 1, :] = jnp.sum(jnp.where(mine, value, 0.0), axis=0, keepdims=True)


def home_kernel(back_ref, slot_ref, source_ref, out_ref):
    sources, _, slots = back_ref.shape
    pairs = slot_ref.shape[1]
    rest = jnp.concatenate([back_ref[:, 0, :], back_ref[:, 1, :]], axis=0)
    parts = []
    for _ in range(3):
        part = rest.astype(jnp.bfloat16)
        rest = rest - part.astype(jnp.float32)
        parts.append(part)
    hot = jnp.where(
        lax.broadcasted_iota(jnp.int32, (slots, pairs), 0) == slot_ref[...], 1.0, 0.0
    ).astype(jnp.bfloat16)
    spread = jnp.dot(jnp.concatenate(parts, axis=0), hot, preferred_element_type=jnp.float32)
    n = 2 * sources
    value = (spread[0:n] + spread[n : 2 * n]) + spread[2 * n : 3 * n]
    mine = lax.broadcasted_iota(jnp.int32, (sources, pairs), 0) == source_ref[...]
    for part in range(2):
        out_ref[part : part + 1, :] = jnp.sum(
            jnp.where(mine, value[part * sources : (part + 1) * sources], 0.0), axis=0, keepdims=True
        )


def params(mebibytes):
    return pltpu.CompilerParams(vmem_limit_bytes=mebibytes * 1024 * 1024)


IN_VMEM = pl.BlockSpec(memory_space=pltpu.VMEM)


def local(propagators, z_sites, z_class, kernel_table, pair_combo, pair_site):
    slabs = lax.axis_size("ta")
    blocks = lax.axis_size("sa")
    me = lax.axis_index("ta")
    rows = propagators.shape[1]
    site_count = propagators.shape[2] // slabs
    z_count = z_sites.shape[0]
    pair_count = pair_site.shape[0]
    classes = kernel_table.shape[0]
    depth = NSC * z_count

    def exchange(array, axis):
        return lax.all_to_all(array, axis, split_axis=0, concat_axis=0, tiled=True)

    lists = jnp.concatenate([z_sites, pair_site, pair_combo[:, 0]]).reshape(1, -1, 128)
    lists = exchange(jnp.broadcast_to(lists, (slabs,) + lists.shape[1:]), "ta")

    one_hot = (
        z_class[None, :] == jnp.arange(kernel_table.shape[1], dtype=jnp.int32)[:, None]
    ).astype(jnp.float32)
    weights = jnp.dot(kernel_table, one_hot, precision=lax.Precision.HIGHEST)

    steps = slabs // 2
    z_rows = pl.pallas_call(
        z_gather_kernel,
        in_specs=[IN_VMEM, pl.BlockSpec(memory_space=pl.ANY), pl.BlockSpec(memory_space=pl.ANY)],
        out_specs=pl.BlockSpec(memory_space=pl.ANY),
        out_shape=jax.ShapeDtypeStruct((slabs, 24, depth), jnp.bfloat16),
        scratch_shapes=[
            pltpu.VMEM((steps, rows, slabs // steps * site_count), jnp.bfloat16),
            pltpu.VMEM((slabs, 24, depth), jnp.bfloat16),
            pltpu.SemaphoreType.DMA((steps,)),
            pltpu.SemaphoreType.DMA((steps,)),
        ],
        compiler_params=params(50),
        cost_estimate=pl.CostEstimate(
            flops=2 * rows * site_count * z_count * slabs, bytes_accessed=15_000_000, transcendentals=0
        ),
        name="z_gather",
    )(lists, propagators, weights)
    z_rows = exchange(z_rows, "ta")

    slots = 128
    partner = pl.pallas_call(
        pair_pick_kernel,
        in_specs=[pl.BlockSpec(memory_space=pltpu.SMEM), IN_VMEM, IN_VMEM],
        out_specs=IN_VMEM,
        out_shape=jax.ShapeDtypeStruct((rows, slabs * slots), jnp.bfloat16),
        compiler_params=params(16),
        cost_estimate=pl.CostEstimate(
            flops=2 * rows * site_count * slots * slabs, bytes_accessed=11_000_000, transcendentals=0
        ),
        name="pair_pick",
    )(me.astype(jnp.int32).reshape(1), lists, propagators)

    combo_ids = pair_combo[:, 0]
    counter = jnp.arange(pair_count, dtype=jnp.int32)
    second = jnp.any(
        (combo_ids[:, None] == combo_ids[None, :]) & (counter[None, :] < counter[:, None]), axis=1
    )
    slot = combo_ids // 256 * 16 + combo_ids % 16 + jnp.where(second, 64, 0)
    slot = slot.reshape(1, -1)
    source = (combo_ids // 16 % 16).reshape(1, -1)

    sums = pl.pallas_call(
        combo_kernel,
        in_specs=[pl.BlockSpec(memory_space=pl.ANY), IN_VMEM] + [pl.BlockSpec(memory_space=pl.ANY)] * 3,
        out_specs=IN_VMEM,
        out_shape=jax.ShapeDtypeStruct((slabs, classes * 40 + 16, 128), jnp.int16),
        scratch_shapes=[
            pltpu.VMEM((3, slabs, 24, depth // 3), jnp.bfloat16),
            pltpu.VMEM((classes * slabs * 24, slabs * 16), jnp.float32),
            pltpu.VMEM((classes * slabs * 8, slabs * 8), jnp.float32),
            pltpu.VMEM((slabs, classes * 40, 128), jnp.float32),
            pltpu.SemaphoreType.DMA((3,)),
        ],
        compiler_params=params(32),
        cost_estimate=pl.CostEstimate(
            flops=2 * classes * 384 * 384 * depth, bytes_accessed=6_000_000, transcendentals=0
        ),
        name="combo_sums",
    )(z_rows, weights, partner, slot, source)

    sums = pl.pallas_call(
        reduce_kernel,
        in_specs=[IN_VMEM],
        out_specs=IN_VMEM,
        out_shape=jax.ShapeDtypeStruct((blocks,) + sums.shape[1:], jnp.int16),
        compiler_params=params(16),
        name="reduce_sums",
    )(exchange(sums, "ta"))
    sums = exchange(sums, "sa")

    found = pl.pallas_call(
        amplitude_kernel,
        in_specs=[IN_VMEM] * 4,
        out_specs=IN_VMEM,
        out_shape=jax.ShapeDtypeStruct((slabs, 2, slots), jnp.float32),
        compiler_params=params(32),
        name="amplitudes",
    )(
        sums,
        jnp.asarray(fold_matrix(), jnp.bfloat16),
        jnp.asarray(spread_matrix(), jnp.bfloat16),
        partner,
    )
    back = exchange(found, "ta")
    return pl.pallas_call(
        home_kernel,
        in_specs=[IN_VMEM] * 3,
        out_specs=IN_VMEM,
        out_shape=jax.ShapeDtypeStruct((2, pair_count), jnp.float32),
        compiler_params=params(16),
        name="home",
    )(back, slot, source)


def solution(mesh):
    placed = (
        P("ta", None, "sa"),
        P(("ta", "sa")),
        P(("ta", "sa")),
        P(),
        P(("ta", "sa"), None),
        P(("ta", "sa")),
    )
    return jax.shard_map(
        local, mesh=mesh, in_specs=placed, out_specs=P(None, ("ta", "sa")), check_vma=False
    )
```

```python
import functools

import jax
import jax.numpy as jnp
import numpy as np
from jax import lax
from jax.experimental import pallas as pl
from jax.experimental.pallas import tpu as pltpu
from jax.sharding import PartitionSpec as P

NSC = 12
MAIN = 384
SENT = 448

def one_hot_columns(idx_row, count):
    rows = lax.broadcasted_iota(jnp.int32, (count, idx_row.shape[1]), 0)
    return jnp.where(rows == idx_row, 1.0, 0.0).astype(jnp.bfloat16)


def doubled(row, upper):
    other = pltpu.roll(row, 64, 1)
    low = lax.broadcasted_iota(jnp.int32, row.shape, 1) < 64
    return jnp.where(low, other, row) if upper else jnp.where(low, row, other)


def as_column(row):
    eye = lax.broadcasted_iota(jnp.int32, (128, 128), 0) == lax.broadcasted_iota(jnp.int32, (128, 128), 1)
    return jnp.sum(jnp.where(eye, row, 0.0), axis=1, keepdims=True)


def list_kernel(z_hbm, site_hbm, combo_hbm, out_ref, z_ref, site_ref, combo_ref, sems):
    copies = [
        pltpu.make_async_copy(source, held, sems.at[k])
        for k, (source, held) in enumerate(((z_hbm, z_ref), (site_hbm, site_ref), (combo_hbm, combo_ref)))
    ]
    for copy in copies:
        copy.start()
    for copy in copies:
        copy.wait()
    groups = z_ref.shape[0]
    row = [z_ref[g : g + 1, :].astype(jnp.float32) for g in range(groups)]
    col = [as_column(r) for r in row]
    sub = lax.broadcasted_iota(jnp.int32, (128, 128), 0)
    lane = lax.broadcasted_iota(jnp.int32, (128, 128), 1)
    first_col, first_row = [], []
    for g in range(groups):
        again_col = jnp.where((col[g] == row[g]) & (lane < sub), 1.0, 0.0)
        again_row = jnp.where((col[g] == row[g]) & (sub < lane), 1.0, 0.0)
        for h in range(g):
            again_col = jnp.maximum(again_col, jnp.where(col[g] == row[h], 1.0, 0.0))
            again_row = jnp.maximum(again_row, jnp.where(col[h] == row[g], 1.0, 0.0))
        first_col.append(1.0 - jnp.max(again_col, axis=1, keepdims=True))
        first_row.append(1.0 - jnp.max(again_row, axis=0, keepdims=True))
    count = jnp.zeros((1, 1), jnp.float32)
    place = []
    for g in range(groups):
        here = jnp.sum(jnp.where(lane < sub, first_row[g], 0.0), axis=1, keepdims=True) + count
        place.append(jnp.where(first_col[g] > 0.5, here, -1.0))
        count = count + jnp.sum(first_row[g], axis=1, keepdims=True)
    block = []
    for g in range(groups):
        want = (lane + 128 * g).astype(jnp.float32)
        total = jnp.zeros((128, 128), jnp.float32)
        for h in range(groups):
            total += jnp.where(place[h] == want, col[h], 0.0)
        found = jnp.sum(total, axis=0, keepdims=True)
        block.append(jnp.where(want[0:1, :] < count, found, -1.0).astype(jnp.int32))
    block += [site_ref[...], combo_ref[...]]
    block.append(jnp.broadcast_to(count, (16 - 3 * groups, 128)).astype(jnp.int32))
    block = jnp.concatenate(block, axis=0)
    for t in range(out_ref.shape[0]):
        out_ref[t] = block


def weight_kernel(w_ref, z_ref, idx_ref, out_ref):
    classes = w_ref.shape[0]
    groups = z_ref.shape[0]
    hot = []
    for g in range(groups):
        col = as_column(z_ref[g : g + 1, :].astype(jnp.float32))
        hot.append(
            jnp.concatenate(
                [
                    jnp.where(col == idx_ref[0, h : h + 1, :].astype(jnp.float32), 1.0, 0.0)
                    for h in range(groups)
                ],
                axis=1,
            )
        )
    hot = jnp.concatenate(hot, axis=0).astype(jnp.bfloat16)
    rest = w_ref[...]
    added = jnp.zeros(rest.shape, jnp.float32)
    for _ in range(3):
        part = rest.astype(jnp.bfloat16)
        rest = rest - part.astype(jnp.float32)
        added += jnp.dot(part, hot, preferred_element_type=jnp.float32)
    edge = added[:, MAIN : MAIN + 128]
    for l in range(NSC):
        out_ref[:, l * MAIN : (l + 1) * MAIN] = added[:, 0:MAIN]
    for k, upper in ((0, False), (1, True)):
        for m in range(NSC // 2):
            at = NSC * (MAIN + 64 * k) + 128 * m
            out_ref[:, at : at + 128] = doubled(edge, upper)


def ordered_rows(picked, l):
    re, im = l * NSC, NSC * NSC + l * NSC
    return jnp.concatenate(
        [picked[re : re + 8], picked[im : im + 8], picked[re + 8 : re + 12], picked[im + 8 : im + 12]],
        axis=0,
    )


def two_to_a_tile(picked, l):
    low = lax.broadcasted_iota(jnp.int32, (24, 128), 1) < 64
    return jnp.where(low, ordered_rows(picked, l), ordered_rows(picked, l + 1)).astype(jnp.bfloat16)


def z_gather_kernel(idx_ref, props_ref, after_ref, out_ref, block_ref, held_ref, in_sems, out_sems):
    slabs = out_ref.shape[0]
    steps = block_ref.shape[0]
    per = slabs // steps
    lanes = block_ref.shape[2]
    sites = lanes // per
    ahead = 3

    def fetch(u):
        at = pl.ds(pl.multiple_of(u * lanes, lanes), lanes)
        return pltpu.make_async_copy(props_ref.at[0, :, at], block_ref.at[u], in_sems.at[u])

    def send(u):
        at = pl.ds(u * per, per)
        return pltpu.make_async_copy(held_ref.at[at], out_ref.at[at], out_sems.at[u])

    for u in range(ahead):
        fetch(u).start()

    def step(u, carry):
        fetch(u).wait()

        @pl.when(u + ahead < steps)
        def _():
            fetch(u + ahead).start()

        for k in range(per):
            t = u * per + k
            idx = idx_ref[t]
            rows = [idx[r : r + 1, :] for r in range(3)] + [doubled(idx[3:4, :], False)]
            hot = jnp.concatenate([one_hot_columns(r, sites) for r in rows], axis=1)
            block = block_ref[u, :, k * sites : (k + 1) * sites]
            picked = jnp.dot(block, hot, preferred_element_type=jnp.float32)
            for l in range(NSC):
                held_ref[t, :, l * MAIN : (l + 1) * MAIN] = ordered_rows(picked[:, 0:MAIN], l).astype(
                    jnp.bfloat16
                )
            for l in range(0, NSC, 2):
                at = NSC * MAIN + 64 * l
                held_ref[t, :, at : at + 128] = two_to_a_tile(picked[:, MAIN : MAIN + 128], l)
        send(u).start()
        return carry

    lax.fori_loop(0, steps, step, 0)
    for u in range(steps):
        send(u).wait()


def rest_gather_kernel(idx_ref, props_ref, out_ref):
    hot = one_hot_columns(doubled(idx_ref[0, 3:4, :], True), props_ref.shape[2])
    picked = jnp.dot(props_ref[0], hot, preferred_element_type=jnp.float32)
    for l in range(0, NSC, 2):
        out_ref[0, :, 64 * l : 64 * l + 128] = two_to_a_tile(picked, l)


def pair_pick_kernel(me_ref, idx_ref, props_ref, out_ref):
    slabs = idx_ref.shape[0]
    sites = props_ref.shape[2] // slabs
    lax.fori_loop(0, slabs, functools.partial(pick_block, me_ref, idx_ref, props_ref, out_ref, sites), 0)


def pick_block(me_ref, idx_ref, props_ref, out_ref, sites, t, carry):
    idx = idx_ref[t]
    far = 1 << 20
    ids = lax.broadcasted_iota(jnp.int32, (64, 128), 0)
    lane = lax.broadcasted_iota(jnp.int32, (1, 128), 1)
    first = jnp.full((64, 128), far, jnp.int32)
    last = jnp.full((64, 128), -1, jnp.int32)
    for r in range(4):
        combo = idx[8 + r : 9 + r, :]
        key = jnp.where(combo // 16 % 16 == me_ref[0], combo // 256 * 16 + combo % 16, -1)
        code = (r * 128 + lane) * sites + idx[4 + r : 5 + r, :]
        mine = ids == key
        first = jnp.minimum(first, jnp.where(mine, code, far))
        last = jnp.maximum(last, jnp.where(mine, code, -1))
    first = jnp.min(first, axis=1, keepdims=True)
    last = jnp.max(last, axis=1, keepdims=True)
    found = jnp.concatenate([first, last], axis=0)
    place = jnp.where((found >= 0) & (found < far), found % sites, -1)
    hot = jnp.where(
        lax.broadcasted_iota(jnp.int32, (128, sites), 1) == place, 1.0, 0.0
    ).astype(jnp.bfloat16)
    block = props_ref[0, :, pl.ds(pl.multiple_of(t * sites, sites), sites)]
    out_ref[:, pl.ds(pl.multiple_of(t * 128, 128), 128)] = lax.dot_general(
        block, hot, (((1,), (1,)), ((), ())), preferred_element_type=jnp.float32
    ).astype(jnp.bfloat16)
    return carry


def coded(sums):
    groups, rows, lanes = sums.shape
    lane = lax.broadcasted_iota(jnp.int32, (groups, lanes), 1)
    tail_row = lax.broadcasted_iota(jnp.int32, (groups, 16, lanes), 1)
    tail = jnp.zeros((groups, 16, lanes), jnp.int32)
    whole = []
    for c in range(rows // 40):
        part = sums[:, 40 * c : 40 * c + 40, :]
        peak = jnp.max(jnp.abs(part), axis=1)
        for d in (4, 2, 1):
            other = jnp.where(
                lane % (2 * d) < d, pltpu.roll(peak, lanes - d, 1), pltpu.roll(peak, d, 1)
            )
            peak = jnp.maximum(peak, other)
        shift = 14.0 - jnp.floor(jnp.log2(jnp.maximum(peak, 2.0**-112)))
        value = jnp.floor(part * jnp.exp2(shift)[:, None, :] + 0.5)
        whole.append(jnp.clip(value, -32767.0, 32767.0).astype(jnp.int32))
        tail = jnp.where(tail_row == c, shift.astype(jnp.int32)[:, None, :], tail)
    return jnp.concatenate(whole + [tail], axis=1).astype(jnp.int16)


def decoded_sum(coded_ref):
    total = None
    for g in range(coded_ref.shape[0]):
        value = coded_ref[g].astype(jnp.int32).astype(jnp.float32)
        rows = value.shape[0] - 16
        parts = []
        for c in range(rows // 40):
            scale = jnp.exp2(-value[rows + c : rows + c + 1, :])
            parts.append(value[40 * c : 40 * c + 40, :] * scale)
        term = jnp.concatenate(parts, axis=0)
        total = term if total is None else total + term
    return total


def combo_kernel(
    more_ref, x_ref, rest_ref, w_ref, after_a, after_b, after_c,
    out_ref, held_ref, rest_held, acc_ref, last_ref, sums_ref, sems,
):
    sources, _, lanes = x_ref.shape
    classes = w_ref.shape[0]
    depth = held_ref.shape[3]
    rest_depth = rest_held.shape[2]
    n = sources * 8

    def piece(s):
        at = pl.ds(pl.multiple_of(s * depth, depth), depth)
        return pltpu.make_async_copy(x_ref.at[:, :, at], held_ref.at[s], sems.at[s])

    for s in range(lanes // depth):
        piece(s).start()

    def products(wide, weights):
        rows = jnp.concatenate(
            [wide[:, 8 * t : 8 * t + 8, :].reshape(n, wide.shape[2]) for t in range(3)], axis=0
        )
        right = rows.astype(jnp.bfloat16)
        scaled = [rows * weights[c : c + 1, :] for c in range(classes)]
        left = jnp.concatenate(
            [scaled[c][n * t : n * t + n, :] for t in range(3) for c in range(classes)], axis=0
        ).astype(jnp.bfloat16)
        contract = (((1,), (1,)), ((), ()))
        main = lax.dot_general(left, right[0 : 2 * n], contract, preferred_element_type=jnp.float32)
        last = lax.dot_general(
            left[2 * classes * n :], right[2 * n :], contract, preferred_element_type=jnp.float32
        )
        return main, last

    def chunk(s, carry):
        piece(s).wait()
        at = pl.ds(pl.multiple_of(s * depth, depth), depth)
        main, last = products(held_ref[s].astype(jnp.float32), w_ref[:, at])

        @pl.when(s == 0)
        def _():
            acc_ref[...] = main
            last_ref[...] = last

        @pl.when(s > 0)
        def _():
            acc_ref[...] += main
            last_ref[...] += last

        return carry

    lax.fori_loop(0, lanes // depth, chunk, 0)

    @pl.when(more_ref[0] > 0)
    def _():
        copy = pltpu.make_async_copy(rest_ref, rest_held, sems.at[lanes // depth])
        copy.start()
        copy.wait()
        main, last = products(rest_held[...].astype(jnp.float32), w_ref[:, lanes : lanes + rest_depth])
        acc_ref[...] += main
        last_ref[...] += last

    low_row = lax.broadcasted_iota(jnp.int32, (n, n), 0) % 8 < 4
    low_lane = lax.broadcasted_iota(jnp.int32, (n, n), 1) % 8 < 4

    def swap_rows(m):
        return pltpu.roll(m.reshape(sources, 8, n), 4, 1).reshape(n, n)

    def swap_lanes(m):
        return jnp.where(low_lane, pltpu.roll(m, n - 4, 1), pltpu.roll(m, 4, 1))

    for c in range(classes):

        def blk(left_tile, right_tile):
            at = (left_tile * classes + c) * n
            return acc_ref[at : at + n, n * right_tile : n * right_tile + n]

        re = (blk(0, 0) + blk(1, 1)).T
        im = (blk(0, 1) - blk(1, 0)).T
        a, b = blk(2, 0), swap_rows(blk(2, 1))
        wide_col = jnp.where(low_row, a + b, b - a).T
        tall_row = jnp.where(low_row, a + b, a - b)
        a = last_ref[c * n : c * n + n, :]
        b = swap_lanes(swap_rows(a))
        corner = jnp.where(low_row, jnp.where(low_lane, a + b, a - b), 0.0).T
        for k, m in enumerate((re, im, wide_col, tall_row, corner)):
            at = (c * 5 + k) * 8
            sums_ref[:, at : at + 8, :] = m.reshape(sources, 8, n)
    out_ref[...] = coded(sums_ref[...])


def reduce_kernel(coded_ref, out_ref):
    total = coded(decoded_sum(coded_ref)[None])
    for g in range(out_ref.shape[0]):
        out_ref[g] = total[0]


def spread_matrix():
    out = np.zeros((5, 8, 8, 768), np.float32)

    def put(k, r, q, j, i, imag):
        at = j * NSC + i
        half = NSC * NSC
        if imag:
            out[k, r, q, half + at] = -1.0
            out[k, r, q, 384 + at] = 1.0
        else:
            out[k, r, q, at] = 1.0
            out[k, r, q, 384 + half + at] = 1.0

    for r in range(8):
        for q in range(8):
            put(0, r, q, r, q, False)
            put(1, r, q, r, q, True)
            put(2, r, q, r, 8 + q % 4, q >= 4)
            put(3, r, q, 8 + r % 4, q, r >= 4)
            if q < 4:
                put(4, r, q, 8 + r % 4, 8 + q, r >= 4)
    return out.reshape(320, 768)


def fold_matrix():
    r = np.arange(1024)[:, None] // 128
    q = np.arange(1024)[:, None] % 8
    return (np.arange(64)[None, :] == r * 8 + q).astype(np.float32)


def amplitude_kernel(sums_ref, fold_ref, spread_ref, partner_ref, out_ref):
    classes, sources = 4, 16
    combos = classes * sources
    sums = decoded_sum(sums_ref)
    own = (
        lax.broadcasted_iota(jnp.int32, (sources, 128), 1) // 8
        == lax.broadcasted_iota(jnp.int32, (sources, 128), 0)
    )
    total = jnp.zeros((2 * combos, 768), jnp.float32)
    for k in range(5):
        tall = []
        for c in range(classes):
            at = (c * 5 + k) * 8
            tall.append(
                jnp.concatenate(
                    [
                        jnp.where(own, jnp.broadcast_to(sums[at + r : at + r + 1, :], (sources, 128)), 0.0)
                        for r in range(8)
                    ],
                    axis=1,
                )
            )
        tall = jnp.concatenate(tall, axis=0)
        high = tall.astype(jnp.bfloat16)
        low = (tall - high.astype(jnp.float32)).astype(jnp.bfloat16)
        both = jnp.concatenate([high, low], axis=0)
        folded = jnp.dot(both, fold_ref[...], preferred_element_type=jnp.float32)
        total += jnp.dot(
            folded.astype(jnp.bfloat16),
            spread_ref[64 * k : 64 * k + 64, :],
            preferred_element_type=jnp.float32,
        )
    rows = partner_ref.shape[0]
    probe = jnp.concatenate([total[:, 0:rows], total[:, 384 : 384 + rows]], axis=0).astype(jnp.bfloat16)
    traces = jnp.dot(probe, partner_ref[...], preferred_element_type=jnp.float32)
    mine = (
        lax.broadcasted_iota(jnp.int32, (combos, 128), 1) % combos
        == lax.broadcasted_iota(jnp.int32, (combos, 128), 0)
    )
    for t in range(out_ref.shape[0]):
        lanes = slice(t * 128, t * 128 + 128)
        for part in range(2):
            at = part * 2 * combos
            value = traces[at : at + combos, lanes] + traces[at + combos : at + 2 * combos, lanes]
            out_ref[t, part : part + 1, :] = jnp.sum(jnp.where(mine, value, 0.0), axis=0, keepdims=True)


def home_kernel(back_ref, slot_ref, source_ref, out_ref):
    sources, _, slots = back_ref.shape
    pairs = slot_ref.shape[1]
    rest = jnp.concatenate([back_ref[:, 0, :], back_ref[:, 1, :]], axis=0)
    parts = []
    for _ in range(3):
        part = rest.astype(jnp.bfloat16)
        rest = rest - part.astype(jnp.float32)
        parts.append(part)
    hot = jnp.where(
        lax.broadcasted_iota(jnp.int32, (slots, pairs), 0) == slot_ref[...], 1.0, 0.0
    ).astype(jnp.bfloat16)
    spread = jnp.dot(jnp.concatenate(parts, axis=0), hot, preferred_element_type=jnp.float32)
    n = 2 * sources
    value = (spread[0:n] + spread[n : 2 * n]) + spread[2 * n : 3 * n]
    mine = lax.broadcasted_iota(jnp.int32, (sources, pairs), 0) == source_ref[...]
    for part in range(2):
        out_ref[part : part + 1, :] = jnp.sum(
            jnp.where(mine, value[part * sources : (part + 1) * sources], 0.0), axis=0, keepdims=True
        )


def params(mebibytes):
    return pltpu.CompilerParams(vmem_limit_bytes=mebibytes * 1024 * 1024)


IN_VMEM = pl.BlockSpec(memory_space=pltpu.VMEM)


def local(propagators, z_sites, z_class, kernel_table, pair_combo, pair_site):
    slabs = lax.axis_size("ta")
    blocks = lax.axis_size("sa")
    me = lax.axis_index("ta")
    rows = propagators.shape[1]
    site_count = propagators.shape[2] // slabs
    z_count = z_sites.shape[0]
    pair_count = pair_site.shape[0]
    classes = kernel_table.shape[0]
    depth = NSC * SENT
    rest_depth = NSC * (z_count - SENT)

    def exchange(array, axis):
        return lax.all_to_all(array, axis, split_axis=0, concat_axis=0, tiled=True)

    z_table = z_sites.reshape(-1, 128)
    lists = pl.pallas_call(
        list_kernel,
        in_specs=[pl.BlockSpec(memory_space=pl.ANY)] * 3,
        out_specs=IN_VMEM,
        out_shape=jax.ShapeDtypeStruct((slabs, 16, 128), jnp.int32),
        scratch_shapes=[pltpu.VMEM((z_count // 128, 128), jnp.int32)] * 3 + [pltpu.SemaphoreType.DMA((3,))],
        compiler_params=params(60),
        name="lists",
    )(z_table, pair_site.reshape(-1, 128), pair_combo.reshape(-1, 128))
    own_list = lists[0:1]
    lists = exchange(lists, "ta")
    more = jnp.any(lists[:, 12, 0] > SENT)

    one_hot = (
        z_class[None, :] == jnp.arange(kernel_table.shape[1], dtype=jnp.int32)[:, None]
    ).astype(jnp.float32)
    weights = jnp.dot(kernel_table, one_hot, precision=lax.Precision.HIGHEST)

    steps = slabs // 2
    z_rows = pl.pallas_call(
        z_gather_kernel,
        in_specs=[IN_VMEM, pl.BlockSpec(memory_space=pl.ANY), pl.BlockSpec(memory_space=pl.ANY)],
        out_specs=pl.BlockSpec(memory_space=pl.ANY),
        out_shape=jax.ShapeDtypeStruct((slabs, 24, depth), jnp.bfloat16),
        scratch_shapes=[
            pltpu.VMEM((steps, rows, slabs // steps * site_count), jnp.bfloat16),
            pltpu.VMEM((slabs, 24, depth), jnp.bfloat16),
            pltpu.SemaphoreType.DMA((steps,)),
            pltpu.SemaphoreType.DMA((steps,)),
        ],
        compiler_params=params(50),
        cost_estimate=pl.CostEstimate(
            flops=2 * rows * site_count * z_count * slabs, bytes_accessed=15_000_000, transcendentals=0
        ),
        name="z_gather",
    )(lists, propagators, weights)
    z_rows = exchange(z_rows, "ta")

    def send_rest(lists, propagators, blank):
        rest = pl.pallas_call(
            rest_gather_kernel,
            grid=(slabs,),
            in_specs=[
                pl.BlockSpec((1,) + lists.shape[1:], lambda t: (t, 0, 0)),
                pl.BlockSpec((1, rows, site_count), lambda t: (0, 0, t)),
            ],
            out_specs=pl.BlockSpec((1, 24, rest_depth), lambda t: (t, 0, 0)),
            out_shape=jax.ShapeDtypeStruct((slabs, 24, rest_depth), jnp.bfloat16),
            compiler_params=params(24),
            name="rest_gather",
        )(lists, propagators)
        return exchange(rest, "ta")

    def no_rest(lists, propagators, blank):
        return blank

    blank = jnp.zeros((slabs, 24, rest_depth), jnp.bfloat16)
    after, blank, z_rows = lax.optimization_barrier((more, blank, z_rows))
    rest_rows = lax.cond(after, send_rest, no_rest, lists, propagators, blank)
    added = pl.pallas_call(
        weight_kernel,
        in_specs=[IN_VMEM] * 3,
        out_specs=IN_VMEM,
        out_shape=jax.ShapeDtypeStruct((classes, depth + rest_depth), jnp.float32),
        compiler_params=params(16),
        name="weights",
    )(weights, z_table, own_list)

    slots = 128
    partner = pl.pallas_call(
        pair_pick_kernel,
        in_specs=[pl.BlockSpec(memory_space=pltpu.SMEM), IN_VMEM, IN_VMEM],
        out_specs=IN_VMEM,
        out_shape=jax.ShapeDtypeStruct((rows, slabs * slots), jnp.bfloat16),
        compiler_params=params(16),
        cost_estimate=pl.CostEstimate(
            flops=2 * rows * site_count * slots * slabs, bytes_accessed=11_000_000, transcendentals=0
        ),
        name="pair_pick",
    )(me.astype(jnp.int32).reshape(1), lists, propagators)

    combo_ids = pair_combo[:, 0]
    counter = jnp.arange(pair_count, dtype=jnp.int32)
    second = jnp.any(
        (combo_ids[:, None] == combo_ids[None, :]) & (counter[None, :] < counter[:, None]), axis=1
    )
    slot = combo_ids // 256 * 16 + combo_ids % 16 + jnp.where(second, 64, 0)
    slot = slot.reshape(1, -1)
    source = (combo_ids // 16 % 16).reshape(1, -1)

    sums = pl.pallas_call(
        combo_kernel,
        in_specs=[
            pl.BlockSpec(memory_space=pltpu.SMEM),
            pl.BlockSpec(memory_space=pl.ANY),
            pl.BlockSpec(memory_space=pl.ANY),
            IN_VMEM,
        ]
        + [pl.BlockSpec(memory_space=pl.ANY)] * 3,
        out_specs=IN_VMEM,
        out_shape=jax.ShapeDtypeStruct((slabs, classes * 40 + 16, 128), jnp.int16),
        scratch_shapes=[
            pltpu.VMEM((3, slabs, 24, depth // 3), jnp.bfloat16),
            pltpu.VMEM((slabs, 24, rest_depth), jnp.bfloat16),
            pltpu.VMEM((classes * slabs * 24, slabs * 16), jnp.float32),
            pltpu.VMEM((classes * slabs * 8, slabs * 8), jnp.float32),
            pltpu.VMEM((slabs, classes * 40, 128), jnp.float32),
            pltpu.SemaphoreType.DMA((4,)),
        ],
        compiler_params=params(32),
        cost_estimate=pl.CostEstimate(
            flops=2 * classes * 384 * 384 * depth, bytes_accessed=6_000_000, transcendentals=0
        ),
        name="combo_sums",
    )(more.astype(jnp.int32).reshape(1), z_rows, rest_rows, added, partner, slot, source)

    sums = pl.pallas_call(
        reduce_kernel,
        in_specs=[IN_VMEM],
        out_specs=IN_VMEM,
        out_shape=jax.ShapeDtypeStruct((blocks,) + sums.shape[1:], jnp.int16),
        compiler_params=params(16),
        name="reduce_sums",
    )(exchange(sums, "ta"))
    sums = exchange(sums, "sa")

    found = pl.pallas_call(
        amplitude_kernel,
        in_specs=[IN_VMEM] * 4,
        out_specs=IN_VMEM,
        out_shape=jax.ShapeDtypeStruct((slabs, 2, slots), jnp.float32),
        compiler_params=params(32),
        name="amplitudes",
    )(
        sums,
        jnp.asarray(fold_matrix(), jnp.bfloat16),
        jnp.asarray(spread_matrix(), jnp.bfloat16),
        partner,
    )
    back = exchange(found, "ta")
    return pl.pallas_call(
        home_kernel,
        in_specs=[IN_VMEM] * 3,
        out_specs=IN_VMEM,
        out_shape=jax.ShapeDtypeStruct((2, pair_count), jnp.float32),
        compiler_params=params(16),
        name="home",
    )(back, slot, source)


def solution(mesh):
    placed = (
        P("ta", None, "sa"),
        P(("ta", "sa")),
        P(("ta", "sa")),
        P(),
        P(("ta", "sa"), None),
        P(("ta", "sa")),
    )
    return jax.shard_map(
        local, mesh=mesh, in_specs=placed, out_specs=P(None, ("ta", "sa")), check_vma=False
    )
```

```python
import functools

import jax
import jax.numpy as jnp
import numpy as np
from jax import lax
from jax.experimental import pallas as pl
from jax.experimental.pallas import tpu as pltpu
from jax.sharding import PartitionSpec as P

NSC = 12
MAIN = 384
SENT = 448

def one_hot_columns(idx_row, count):
    rows = lax.broadcasted_iota(jnp.int32, (count, idx_row.shape[1]), 0)
    return jnp.where(rows == idx_row, 1.0, 0.0).astype(jnp.bfloat16)


def doubled(row, upper):
    other = pltpu.roll(row, 64, 1)
    low = lax.broadcasted_iota(jnp.int32, row.shape, 1) < 64
    return jnp.where(low, other, row) if upper else jnp.where(low, row, other)


def as_column(row):
    eye = lax.broadcasted_iota(jnp.int32, (128, 128), 0) == lax.broadcasted_iota(jnp.int32, (128, 128), 1)
    return jnp.sum(jnp.where(eye, row, 0.0), axis=1, keepdims=True)


def list_kernel(z_hbm, site_hbm, combo_hbm, out_ref, z_ref, site_ref, combo_ref, sems):
    copies = [
        pltpu.make_async_copy(source, held, sems.at[k])
        for k, (source, held) in enumerate(((z_hbm, z_ref), (site_hbm, site_ref), (combo_hbm, combo_ref)))
    ]
    for copy in copies:
        copy.start()
    for copy in copies:
        copy.wait()
    groups = z_ref.shape[0]
    row = [z_ref[g : g + 1, :].astype(jnp.float32) for g in range(groups)]
    col = [as_column(r) for r in row]
    sub = lax.broadcasted_iota(jnp.int32, (128, 128), 0)
    lane = lax.broadcasted_iota(jnp.int32, (128, 128), 1)
    first_col, first_row = [], []
    for g in range(groups):
        again_col = jnp.where((col[g] == row[g]) & (lane < sub), 1.0, 0.0)
        again_row = jnp.where((col[g] == row[g]) & (sub < lane), 1.0, 0.0)
        for h in range(g):
            again_col = jnp.maximum(again_col, jnp.where(col[g] == row[h], 1.0, 0.0))
            again_row = jnp.maximum(again_row, jnp.where(col[h] == row[g], 1.0, 0.0))
        first_col.append(1.0 - jnp.max(again_col, axis=1, keepdims=True))
        first_row.append(1.0 - jnp.max(again_row, axis=0, keepdims=True))
    count = jnp.zeros((1, 1), jnp.float32)
    place = []
    for g in range(groups):
        here = jnp.sum(jnp.where(lane < sub, first_row[g], 0.0), axis=1, keepdims=True) + count
        place.append(jnp.where(first_col[g] > 0.5, here, -1.0))
        count = count + jnp.sum(first_row[g], axis=1, keepdims=True)
    block = []
    for g in range(groups):
        want = (lane + 128 * g).astype(jnp.float32)
        total = jnp.zeros((128, 128), jnp.float32)
        for h in range(groups):
            total += jnp.where(place[h] == want, col[h], 0.0)
        found = jnp.sum(total, axis=0, keepdims=True)
        block.append(jnp.where(want[0:1, :] < count, found, -1.0).astype(jnp.int32))
    block += [site_ref[...], combo_ref[...]]
    block.append(jnp.broadcast_to(count, (16 - 3 * groups, 128)).astype(jnp.int32))
    block = jnp.concatenate(block, axis=0)
    for t in range(out_ref.shape[0]):
        out_ref[t] = block


def weight_kernel(w_ref, z_ref, idx_ref, out_ref):
    classes = w_ref.shape[0]
    groups = z_ref.shape[0]
    hot = []
    for g in range(groups):
        col = as_column(z_ref[g : g + 1, :].astype(jnp.float32))
        hot.append(
            jnp.concatenate(
                [
                    jnp.where(col == idx_ref[0, h : h + 1, :].astype(jnp.float32), 1.0, 0.0)
                    for h in range(groups)
                ],
                axis=1,
            )
        )
    hot = jnp.concatenate(hot, axis=0).astype(jnp.bfloat16)
    rest = w_ref[...]
    added = jnp.zeros(rest.shape, jnp.float32)
    for _ in range(3):
        part = rest.astype(jnp.bfloat16)
        rest = rest - part.astype(jnp.float32)
        added += jnp.dot(part, hot, preferred_element_type=jnp.float32)
    edge = added[:, MAIN : MAIN + 128]
    for l in range(NSC):
        out_ref[:, l * MAIN : (l + 1) * MAIN] = added[:, 0:MAIN]
    for k, upper in ((0, False), (1, True)):
        for m in range(NSC // 2):
            at = NSC * (MAIN + 64 * k) + 128 * m
            out_ref[:, at : at + 128] = doubled(edge, upper)


def ordered_rows(picked, l):
    re, im = l * NSC, NSC * NSC + l * NSC
    return jnp.concatenate(
        [picked[re : re + 8], picked[im : im + 8], picked[re + 8 : re + 12], picked[im + 8 : im + 12]],
        axis=0,
    )


def two_to_a_tile(picked, l):
    low = lax.broadcasted_iota(jnp.int32, (24, 128), 1) < 64
    return jnp.where(low, ordered_rows(picked, l), ordered_rows(picked, l + 1)).astype(jnp.bfloat16)


def pick_sites(block, rows):
    count, half = block.shape[0], block.shape[1] // 2
    hot = jnp.concatenate([one_hot_columns(r % half, half) for r in rows], axis=1)
    upper = jnp.concatenate(rows, axis=1) >= half
    both = jnp.concatenate([block[:, 0:half], block[:, half:]], axis=0)
    picked = jnp.dot(both, hot, preferred_element_type=jnp.float32)
    return jnp.where(upper, picked[count:], picked[0:count])


def z_gather_kernel(idx_ref, props_ref, after_ref, out_ref, block_ref, held_ref, in_sems, out_sems):
    slabs = out_ref.shape[0]
    steps = block_ref.shape[0]
    per = slabs // steps
    lanes = block_ref.shape[2]
    sites = lanes // per
    ahead = min(3, steps)

    def fetch(u):
        at = pl.ds(pl.multiple_of(u * lanes, lanes), lanes)
        return pltpu.make_async_copy(props_ref.at[0, :, at], block_ref.at[u], in_sems.at[u])

    def send(u):
        at = pl.ds(u * per, per)
        return pltpu.make_async_copy(held_ref.at[at], out_ref.at[at], out_sems.at[u])

    for u in range(ahead):
        fetch(u).start()

    def step(u, carry):
        fetch(u).wait()

        @pl.when(u + ahead < steps)
        def _():
            fetch(u + ahead).start()

        for k in range(per):
            t = u * per + k
            idx = idx_ref[t]
            rows = [idx[r : r + 1, :] for r in range(3)] + [doubled(idx[3:4, :], False)]
            picked = pick_sites(block_ref[u, :, k * sites : (k + 1) * sites], rows)
            for l in range(NSC):
                held_ref[t, :, l * MAIN : (l + 1) * MAIN] = ordered_rows(picked[:, 0:MAIN], l).astype(
                    jnp.bfloat16
                )
            for l in range(0, NSC, 2):
                at = NSC * MAIN + 64 * l
                held_ref[t, :, at : at + 128] = two_to_a_tile(picked[:, MAIN : MAIN + 128], l)
        send(u).start()
        return carry

    lax.fori_loop(0, steps, step, 0)
    for u in range(steps):
        send(u).wait()


def rest_gather_kernel(idx_ref, props_ref, out_ref):
    hot = one_hot_columns(doubled(idx_ref[0, 3:4, :], True), props_ref.shape[2])
    picked = jnp.dot(props_ref[0], hot, preferred_element_type=jnp.float32)
    for l in range(0, NSC, 2):
        out_ref[0, :, 64 * l : 64 * l + 128] = two_to_a_tile(picked, l)


def pair_pick_kernel(me_ref, idx_ref, props_ref, out_ref):
    slabs = idx_ref.shape[0]
    sites = props_ref.shape[2] // slabs
    lax.fori_loop(0, slabs, functools.partial(pick_block, me_ref, idx_ref, props_ref, out_ref, sites), 0)


def pick_block(me_ref, idx_ref, props_ref, out_ref, sites, t, carry):
    idx = idx_ref[t]
    far = 1 << 20
    ids = lax.broadcasted_iota(jnp.int32, (64, 128), 0)
    lane = lax.broadcasted_iota(jnp.int32, (1, 128), 1)
    first = jnp.full((64, 128), far, jnp.int32)
    last = jnp.full((64, 128), -1, jnp.int32)
    for r in range(4):
        combo = idx[8 + r : 9 + r, :]
        key = jnp.where(combo // 16 % 16 == me_ref[0], combo // 256 * 16 + combo % 16, -1)
        code = (r * 128 + lane) * sites + idx[4 + r : 5 + r, :]
        mine = ids == key
        first = jnp.minimum(first, jnp.where(mine, code, far))
        last = jnp.maximum(last, jnp.where(mine, code, -1))
    first = jnp.min(first, axis=1, keepdims=True)
    last = jnp.max(last, axis=1, keepdims=True)
    found = jnp.concatenate([first, last], axis=0)
    place = jnp.where((found >= 0) & (found < far), found % sites, -1)
    hot = jnp.where(
        lax.broadcasted_iota(jnp.int32, (128, sites), 1) == place, 1.0, 0.0
    ).astype(jnp.bfloat16)
    block = props_ref[0, :, pl.ds(pl.multiple_of(t * sites, sites), sites)]
    out_ref[:, pl.ds(pl.multiple_of(t * 128, 128), 128)] = lax.dot_general(
        block, hot, (((1,), (1,)), ((), ())), preferred_element_type=jnp.float32
    ).astype(jnp.bfloat16)
    return carry


def coded(sums):
    groups, rows, lanes = sums.shape
    lane = lax.broadcasted_iota(jnp.int32, (groups, lanes), 1)
    tail_row = lax.broadcasted_iota(jnp.int32, (groups, 16, lanes), 1)
    tail = jnp.zeros((groups, 16, lanes), jnp.int32)
    whole, corners = [], []
    for c in range(rows // 40):
        part = sums[:, 40 * c : 40 * c + 40, :]
        peak = jnp.max(jnp.abs(part), axis=1)
        for d in (4, 2, 1):
            other = jnp.where(
                lane % (2 * d) < d, pltpu.roll(peak, lanes - d, 1), pltpu.roll(peak, d, 1)
            )
            peak = jnp.maximum(peak, other)
        shift = 14.0 - jnp.floor(jnp.log2(jnp.maximum(peak, 2.0**-112)))
        value = jnp.floor(part * jnp.exp2(shift)[:, None, :] + 0.5)
        value = jnp.clip(value, -32767.0, 32767.0)
        whole.append(value[:, 0:32, :].astype(jnp.int32))
        corner = value[:, 32:40, :]
        if c % 2:
            corners.append((even + pltpu.roll(corner, 4, 2)).astype(jnp.int32))
        even = corner
        tail = jnp.where(tail_row == c, shift.astype(jnp.int32)[:, None, :], tail)
    return jnp.concatenate(whole + corners + [tail], axis=1).astype(jnp.int16)


def decoded_sum(coded_ref):
    total = None
    for g in range(coded_ref.shape[0]):
        value = coded_ref[g].astype(jnp.int32).astype(jnp.float32)
        rows, lanes = value.shape
        low = lax.broadcasted_iota(jnp.int32, (8, lanes), 1) % 8 < 4
        classes = (rows - 16) // 36
        parts = []
        for c in range(classes):
            scale = jnp.exp2(-value[rows - 16 + c : rows - 15 + c, :])
            at = 32 * classes + 8 * (c // 2)
            corner = value[at : at + 8, :]
            if c % 2:
                corner = pltpu.roll(corner, lanes - 4, 1)
            parts.append(value[32 * c : 32 * c + 32, :] * scale)
            parts.append(jnp.where(low, corner * scale, 0.0))
        term = jnp.concatenate(parts, axis=0)
        total = term if total is None else total + term
    return total


def combo_kernel(
    more_ref, x_ref, rest_ref, w_ref, after_a, after_b, after_c,
    out_ref, held_ref, rest_held, acc_ref, last_ref, sums_ref, sems,
):
    sources, _, lanes = x_ref.shape
    classes = w_ref.shape[0]
    depth = held_ref.shape[3]
    rest_depth = rest_held.shape[2]
    n = sources * 8

    def piece(s):
        at = pl.ds(pl.multiple_of(s * depth, depth), depth)
        return pltpu.make_async_copy(x_ref.at[:, :, at], held_ref.at[s], sems.at[s])

    for s in range(lanes // depth):
        piece(s).start()

    def products(wide, weights):
        rows = jnp.concatenate(
            [wide[:, 8 * t : 8 * t + 8, :].reshape(n, wide.shape[2]) for t in range(3)], axis=0
        )
        right = rows.astype(jnp.bfloat16)
        scaled = [rows * weights[c : c + 1, :] for c in range(classes)]
        left = jnp.concatenate(
            [scaled[c][n * t : n * t + n, :] for t in range(3) for c in range(classes)], axis=0
        ).astype(jnp.bfloat16)
        contract = (((1,), (1,)), ((), ()))
        main = lax.dot_general(left, right[0 : 2 * n], contract, preferred_element_type=jnp.float32)
        last = lax.dot_general(
            left[2 * classes * n :], right[2 * n :], contract, preferred_element_type=jnp.float32
        )
        return main, last

    def chunk(s, carry):
        piece(s).wait()
        at = pl.ds(pl.multiple_of(s * depth, depth), depth)
        main, last = products(held_ref[s].astype(jnp.float32), w_ref[:, at])

        @pl.when(s == 0)
        def _():
            acc_ref[...] = main
            last_ref[...] = last

        @pl.when(s > 0)
        def _():
            acc_ref[...] += main
            last_ref[...] += last

        return carry

    lax.fori_loop(0, lanes // depth, chunk, 0)

    @pl.when(more_ref[0] > 0)
    def _():
        copy = pltpu.make_async_copy(rest_ref, rest_held, sems.at[lanes // depth])
        copy.start()
        copy.wait()
        main, last = products(rest_held[...].astype(jnp.float32), w_ref[:, lanes : lanes + rest_depth])
        acc_ref[...] += main
        last_ref[...] += last

    low_row = lax.broadcasted_iota(jnp.int32, (n, n), 0) % 8 < 4
    low_lane = lax.broadcasted_iota(jnp.int32, (n, n), 1) % 8 < 4

    def swap_rows(m):
        return pltpu.roll(m.reshape(sources, 8, n), 4, 1).reshape(n, n)

    def swap_lanes(m):
        return jnp.where(low_lane, pltpu.roll(m, n - 4, 1), pltpu.roll(m, 4, 1))

    for c in range(classes):

        def blk(left_tile, right_tile):
            at = (left_tile * classes + c) * n
            return acc_ref[at : at + n, n * right_tile : n * right_tile + n]

        re = (blk(0, 0) + blk(1, 1)).T
        im = (blk(0, 1) - blk(1, 0)).T
        a, b = blk(2, 0), swap_rows(blk(2, 1))
        wide_col = jnp.where(low_row, a + b, b - a).T
        tall_row = jnp.where(low_row, a + b, a - b)
        a = last_ref[c * n : c * n + n, :]
        b = swap_lanes(swap_rows(a))
        corner = jnp.where(low_row, jnp.where(low_lane, a + b, a - b), 0.0).T
        for k, m in enumerate((re, im, wide_col, tall_row, corner)):
            at = (c * 5 + k) * 8
            sums_ref[:, at : at + 8, :] = m.reshape(sources, 8, n)
    out_ref[...] = coded(sums_ref[...])


def reduce_kernel(coded_ref, out_ref):
    total = coded(decoded_sum(coded_ref)[None])
    for g in range(out_ref.shape[0]):
        out_ref[g] = total[0]


def spread_matrix():
    out = np.zeros((5, 8, 8, 768), np.float32)

    def put(k, r, q, j, i, imag):
        at = j * NSC + i
        half = NSC * NSC
        if imag:
            out[k, r, q, half + at] = -1.0
            out[k, r, q, 384 + at] = 1.0
        else:
            out[k, r, q, at] = 1.0
            out[k, r, q, 384 + half + at] = 1.0

    for r in range(8):
        for q in range(8):
            put(0, r, q, r, q, False)
            put(1, r, q, r, q, True)
            put(2, r, q, r, 8 + q % 4, q >= 4)
            put(3, r, q, 8 + r % 4, q, r >= 4)
            if q < 4:
                put(4, r, q, 8 + r % 4, 8 + q, r >= 4)
    return out.reshape(320, 768)


def fold_matrix():
    r = np.arange(1024)[:, None] // 128
    q = np.arange(1024)[:, None] % 8
    return (np.arange(64)[None, :] == r * 8 + q).astype(np.float32)


def amplitude_kernel(sums_ref, fold_ref, spread_ref, partner_ref, out_ref):
    classes, sources = 4, 16
    combos = classes * sources
    sums = decoded_sum(sums_ref)
    own = (
        lax.broadcasted_iota(jnp.int32, (sources, 128), 1) // 8
        == lax.broadcasted_iota(jnp.int32, (sources, 128), 0)
    )
    total = jnp.zeros((2 * combos, 768), jnp.float32)
    for k in range(5):
        tall = []
        for c in range(classes):
            at = (c * 5 + k) * 8
            tall.append(
                jnp.concatenate(
                    [
                        jnp.where(own, jnp.broadcast_to(sums[at + r : at + r + 1, :], (sources, 128)), 0.0)
                        for r in range(8)
                    ],
                    axis=1,
                )
            )
        tall = jnp.concatenate(tall, axis=0)
        high = tall.astype(jnp.bfloat16)
        low = (tall - high.astype(jnp.float32)).astype(jnp.bfloat16)
        both = jnp.concatenate([high, low], axis=0)
        folded = jnp.dot(both, fold_ref[...], preferred_element_type=jnp.float32)
        total += jnp.dot(
            folded.astype(jnp.bfloat16),
            spread_ref[64 * k : 64 * k + 64, :],
            preferred_element_type=jnp.float32,
        )
    rows = partner_ref.shape[0]
    probe = jnp.concatenate([total[:, 0:rows], total[:, 384 : 384 + rows]], axis=0).astype(jnp.bfloat16)
    traces = jnp.dot(probe, partner_ref[...], preferred_element_type=jnp.float32)
    mine = (
        lax.broadcasted_iota(jnp.int32, (combos, 128), 1) % combos
        == lax.broadcasted_iota(jnp.int32, (combos, 128), 0)
    )
    for t in range(out_ref.shape[0]):
        lanes = slice(t * 128, t * 128 + 128)
        for part in range(2):
            at = part * 2 * combos
            value = traces[at : at + combos, lanes] + traces[at + combos : at + 2 * combos, lanes]
            out_ref[t, part : part + 1, :] = jnp.sum(jnp.where(mine, value, 0.0), axis=0, keepdims=True)


def home_kernel(back_ref, slot_ref, source_ref, out_ref):
    sources, _, slots = back_ref.shape
    pairs = slot_ref.shape[1]
    rest = jnp.concatenate([back_ref[:, 0, :], back_ref[:, 1, :]], axis=0)
    parts = []
    for _ in range(3):
        part = rest.astype(jnp.bfloat16)
        rest = rest - part.astype(jnp.float32)
        parts.append(part)
    hot = jnp.where(
        lax.broadcasted_iota(jnp.int32, (slots, pairs), 0) == slot_ref[...], 1.0, 0.0
    ).astype(jnp.bfloat16)
    spread = jnp.dot(jnp.concatenate(parts, axis=0), hot, preferred_element_type=jnp.float32)
    n = 2 * sources
    value = (spread[0:n] + spread[n : 2 * n]) + spread[2 * n : 3 * n]
    mine = lax.broadcasted_iota(jnp.int32, (sources, pairs), 0) == source_ref[...]
    for part in range(2):
        out_ref[part : part + 1, :] = jnp.sum(
            jnp.where(mine, value[part * sources : (part + 1) * sources], 0.0), axis=0, keepdims=True
        )


def params(mebibytes):
    return pltpu.CompilerParams(vmem_limit_bytes=mebibytes * 1024 * 1024)


IN_VMEM = pl.BlockSpec(memory_space=pltpu.VMEM)


def local(propagators, z_sites, z_class, kernel_table, pair_combo, pair_site):
    slabs = lax.axis_size("ta")
    blocks = lax.axis_size("sa")
    me = lax.axis_index("ta")
    rows = propagators.shape[1]
    site_count = propagators.shape[2] // slabs
    z_count = z_sites.shape[0]
    pair_count = pair_site.shape[0]
    classes = kernel_table.shape[0]
    depth = NSC * SENT
    rest_depth = NSC * (z_count - SENT)

    def exchange(array, axis):
        return lax.all_to_all(array, axis, split_axis=0, concat_axis=0, tiled=True)

    z_table = z_sites.reshape(-1, 128)
    lists = pl.pallas_call(
        list_kernel,
        in_specs=[pl.BlockSpec(memory_space=pl.ANY)] * 3,
        out_specs=IN_VMEM,
        out_shape=jax.ShapeDtypeStruct((slabs, 16, 128), jnp.int32),
        scratch_shapes=[pltpu.VMEM((z_count // 128, 128), jnp.int32)] * 3 + [pltpu.SemaphoreType.DMA((3,))],
        compiler_params=params(60),
        name="lists",
    )(z_table, pair_site.reshape(-1, 128), pair_combo.reshape(-1, 128))
    own_list = lists[0:1]
    lists = exchange(lists, "ta")
    more = jnp.any(lists[:, 12, 0] > SENT)

    one_hot = (
        z_class[None, :] == jnp.arange(kernel_table.shape[1], dtype=jnp.int32)[:, None]
    ).astype(jnp.float32)
    weights = jnp.dot(kernel_table, one_hot, precision=lax.Precision.HIGHEST)

    steps = slabs // 4
    z_rows = pl.pallas_call(
        z_gather_kernel,
        in_specs=[IN_VMEM, pl.BlockSpec(memory_space=pl.ANY), pl.BlockSpec(memory_space=pl.ANY)],
        out_specs=pl.BlockSpec(memory_space=pl.ANY),
        out_shape=jax.ShapeDtypeStruct((slabs, 24, depth), jnp.bfloat16),
        scratch_shapes=[
            pltpu.VMEM((steps, rows, slabs // steps * site_count), jnp.bfloat16),
            pltpu.VMEM((slabs, 24, depth), jnp.bfloat16),
            pltpu.SemaphoreType.DMA((steps,)),
            pltpu.SemaphoreType.DMA((steps,)),
        ],
        compiler_params=params(50),
        cost_estimate=pl.CostEstimate(
            flops=2 * rows * site_count * z_count * slabs, bytes_accessed=15_000_000, transcendentals=0
        ),
        name="z_gather",
    )(lists, propagators, weights)
    z_rows = exchange(z_rows, "ta")

    def send_rest(lists, propagators, blank):
        rest = pl.pallas_call(
            rest_gather_kernel,
            grid=(slabs,),
            in_specs=[
                pl.BlockSpec((1,) + lists.shape[1:], lambda t: (t, 0, 0)),
                pl.BlockSpec((1, rows, site_count), lambda t: (0, 0, t)),
            ],
            out_specs=pl.BlockSpec((1, 24, rest_depth), lambda t: (t, 0, 0)),
            out_shape=jax.ShapeDtypeStruct((slabs, 24, rest_depth), jnp.bfloat16),
            compiler_params=params(24),
            name="rest_gather",
        )(lists, propagators)
        return exchange(rest, "ta")

    def no_rest(lists, propagators, blank):
        return blank

    blank = jnp.zeros((slabs, 24, rest_depth), jnp.bfloat16)
    after, blank, z_rows = lax.optimization_barrier((more, blank, z_rows))
    rest_rows = lax.cond(after, send_rest, no_rest, lists, propagators, blank)
    added = pl.pallas_call(
        weight_kernel,
        in_specs=[IN_VMEM] * 3,
        out_specs=IN_VMEM,
        out_shape=jax.ShapeDtypeStruct((classes, depth + rest_depth), jnp.float32),
        compiler_params=params(16),
        name="weights",
    )(weights, z_table, own_list)

    slots = 128
    partner = pl.pallas_call(
        pair_pick_kernel,
        in_specs=[pl.BlockSpec(memory_space=pltpu.SMEM), IN_VMEM, IN_VMEM],
        out_specs=IN_VMEM,
        out_shape=jax.ShapeDtypeStruct((rows, slabs * slots), jnp.bfloat16),
        compiler_params=params(16),
        cost_estimate=pl.CostEstimate(
            flops=2 * rows * site_count * slots * slabs, bytes_accessed=11_000_000, transcendentals=0
        ),
        name="pair_pick",
    )(me.astype(jnp.int32).reshape(1), lists, propagators)

    combo_ids = pair_combo[:, 0]
    counter = jnp.arange(pair_count, dtype=jnp.int32)
    second = jnp.any(
        (combo_ids[:, None] == combo_ids[None, :]) & (counter[None, :] < counter[:, None]), axis=1
    )
    slot = combo_ids // 256 * 16 + combo_ids % 16 + jnp.where(second, 64, 0)
    slot = slot.reshape(1, -1)
    source = (combo_ids // 16 % 16).reshape(1, -1)

    sums = pl.pallas_call(
        combo_kernel,
        in_specs=[
            pl.BlockSpec(memory_space=pltpu.SMEM),
            pl.BlockSpec(memory_space=pl.ANY),
            pl.BlockSpec(memory_space=pl.ANY),
            IN_VMEM,
        ]
        + [pl.BlockSpec(memory_space=pl.ANY)] * 3,
        out_specs=IN_VMEM,
        out_shape=jax.ShapeDtypeStruct((slabs, classes * 36 + 16, 128), jnp.int16),
        scratch_shapes=[
            pltpu.VMEM((3, slabs, 24, depth // 3), jnp.bfloat16),
            pltpu.VMEM((slabs, 24, rest_depth), jnp.bfloat16),
            pltpu.VMEM((classes * slabs * 24, slabs * 16), jnp.float32),
            pltpu.VMEM((classes * slabs * 8, slabs * 8), jnp.float32),
            pltpu.VMEM((slabs, classes * 40, 128), jnp.float32),
            pltpu.SemaphoreType.DMA((4,)),
        ],
        compiler_params=params(32),
        cost_estimate=pl.CostEstimate(
            flops=2 * classes * 384 * 384 * depth, bytes_accessed=6_000_000, transcendentals=0
        ),
        name="combo_sums",
    )(more.astype(jnp.int32).reshape(1), z_rows, rest_rows, added, partner, slot, source)

    sums = pl.pallas_call(
        reduce_kernel,
        in_specs=[IN_VMEM],
        out_specs=IN_VMEM,
        out_shape=jax.ShapeDtypeStruct((blocks,) + sums.shape[1:], jnp.int16),
        compiler_params=params(16),
        name="reduce_sums",
    )(exchange(sums, "ta"))
    sums = exchange(sums, "sa")

    found = pl.pallas_call(
        amplitude_kernel,
        in_specs=[IN_VMEM] * 4,
        out_specs=IN_VMEM,
        out_shape=jax.ShapeDtypeStruct((slabs, 2, slots), jnp.float32),
        compiler_params=params(32),
        name="amplitudes",
    )(
        sums,
        jnp.asarray(fold_matrix(), jnp.bfloat16),
        jnp.asarray(spread_matrix(), jnp.bfloat16),
        partner,
    )
    back = exchange(found, "ta")
    return pl.pallas_call(
        home_kernel,
        in_specs=[IN_VMEM] * 3,
        out_specs=IN_VMEM,
        out_shape=jax.ShapeDtypeStruct((2, pair_count), jnp.float32),
        compiler_params=params(16),
        name="home",
    )(back, slot, source)


def solution(mesh):
    placed = (
        P("ta", None, "sa"),
        P(("ta", "sa")),
        P(("ta", "sa")),
        P(),
        P(("ta", "sa"), None),
        P(("ta", "sa")),
    )
    return jax.shard_map(
        local, mesh=mesh, in_specs=placed, out_specs=P(None, ("ta", "sa")), check_vma=False
    )
```

```python
import functools

import jax
import jax.numpy as jnp
import numpy as np
from jax import lax
from jax.experimental import pallas as pl
from jax.experimental.pallas import tpu as pltpu
from jax.sharding import PartitionSpec as P

NSC = 12
MAIN = 384
SENT = 448

def one_hot_columns(idx_row, count):
    rows = lax.broadcasted_iota(jnp.int32, (count, idx_row.shape[1]), 0)
    return jnp.where(rows == idx_row, 1.0, 0.0).astype(jnp.bfloat16)


def doubled(row, upper):
    other = pltpu.roll(row, 64, 1)
    low = lax.broadcasted_iota(jnp.int32, row.shape, 1) < 64
    return jnp.where(low, other, row) if upper else jnp.where(low, row, other)


def as_column(row):
    eye = lax.broadcasted_iota(jnp.int32, (128, 128), 0) == lax.broadcasted_iota(jnp.int32, (128, 128), 1)
    return jnp.sum(jnp.where(eye, row, 0.0), axis=1, keepdims=True)


def list_kernel(z_hbm, site_hbm, combo_hbm, out_ref, z_ref, site_ref, combo_ref, sems):
    copies = [
        pltpu.make_async_copy(source, held, sems.at[k])
        for k, (source, held) in enumerate(((z_hbm, z_ref), (site_hbm, site_ref), (combo_hbm, combo_ref)))
    ]
    for copy in copies:
        copy.start()
    for copy in copies:
        copy.wait()
    groups = z_ref.shape[0]
    row = [z_ref[g : g + 1, :].astype(jnp.float32) for g in range(groups)]
    col = [as_column(r) for r in row]
    sub = lax.broadcasted_iota(jnp.int32, (128, 128), 0)
    lane = lax.broadcasted_iota(jnp.int32, (128, 128), 1)
    first_col, first_row = [], []
    for g in range(groups):
        again_col = jnp.where((col[g] == row[g]) & (lane < sub), 1.0, 0.0)
        again_row = jnp.where((col[g] == row[g]) & (sub < lane), 1.0, 0.0)
        for h in range(g):
            again_col = jnp.maximum(again_col, jnp.where(col[g] == row[h], 1.0, 0.0))
            again_row = jnp.maximum(again_row, jnp.where(col[h] == row[g], 1.0, 0.0))
        first_col.append(1.0 - jnp.max(again_col, axis=1, keepdims=True))
        first_row.append(1.0 - jnp.max(again_row, axis=0, keepdims=True))
    count = jnp.zeros((1, 1), jnp.float32)
    place = []
    for g in range(groups):
        here = jnp.sum(jnp.where(lane < sub, first_row[g], 0.0), axis=1, keepdims=True) + count
        place.append(jnp.where(first_col[g] > 0.5, here, -1.0))
        count = count + jnp.sum(first_row[g], axis=1, keepdims=True)
    block = []
    for g in range(groups):
        want = (lane + 128 * g).astype(jnp.float32)
        total = jnp.zeros((128, 128), jnp.float32)
        for h in range(groups):
            total += jnp.where(place[h] == want, col[h], 0.0)
        found = jnp.sum(total, axis=0, keepdims=True)
        block.append(jnp.where(want[0:1, :] < count, found, -1.0).astype(jnp.int32))
    block += [site_ref[...], combo_ref[...]]
    block.append(jnp.broadcast_to(count, (16 - 3 * groups, 128)).astype(jnp.int32))
    block = jnp.concatenate(block, axis=0)
    for t in range(out_ref.shape[0]):
        out_ref[t] = block


def weight_kernel(w_ref, z_ref, idx_ref, out_ref):
    classes = w_ref.shape[0]
    groups = z_ref.shape[0]
    hot = []
    for g in range(groups):
        col = as_column(z_ref[g : g + 1, :].astype(jnp.float32))
        hot.append(
            jnp.concatenate(
                [
                    jnp.where(col == idx_ref[0, h : h + 1, :].astype(jnp.float32), 1.0, 0.0)
                    for h in range(groups)
                ],
                axis=1,
            )
        )
    hot = jnp.concatenate(hot, axis=0).astype(jnp.bfloat16)
    rest = w_ref[...]
    added = jnp.zeros(rest.shape, jnp.float32)
    for _ in range(3):
        part = rest.astype(jnp.bfloat16)
        rest = rest - part.astype(jnp.float32)
        added += jnp.dot(part, hot, preferred_element_type=jnp.float32)
    edge = added[:, MAIN : MAIN + 128]
    for l in range(NSC):
        out_ref[:, l * MAIN : (l + 1) * MAIN] = added[:, 0:MAIN]
    for k, upper in ((0, False), (1, True)):
        for m in range(NSC // 2):
            at = NSC * (MAIN + 64 * k) + 128 * m
            out_ref[:, at : at + 128] = doubled(edge, upper)


def ordered_rows(picked, l):
    re, im = l * NSC, NSC * NSC + l * NSC
    return jnp.concatenate(
        [picked[re : re + 8], picked[im : im + 8], picked[re + 8 : re + 12], picked[im + 8 : im + 12]],
        axis=0,
    )


def two_to_a_tile(picked, l):
    low = lax.broadcasted_iota(jnp.int32, (24, 128), 1) < 64
    return jnp.where(low, ordered_rows(picked, l), ordered_rows(picked, l + 1)).astype(jnp.bfloat16)


def pick_sites(block, rows):
    count, half = block.shape[0], block.shape[1] // 2
    hot = jnp.concatenate([one_hot_columns(r % half, half) for r in rows], axis=1)
    upper = jnp.concatenate(rows, axis=1) >= half
    both = jnp.concatenate([block[:, 0:half], block[:, half:]], axis=0)
    picked = jnp.dot(both, hot, preferred_element_type=jnp.float32)
    return jnp.where(upper, picked[count:], picked[0:count])


def z_gather_kernel(idx_ref, props_ref, after_ref, out_ref, block_ref, held_ref, in_sems, out_sems):
    slabs = out_ref.shape[0]
    steps = block_ref.shape[0]
    per = slabs // steps
    lanes = block_ref.shape[2]
    sites = lanes // per
    ahead = min(3, steps)

    def fetch(u):
        at = pl.ds(pl.multiple_of(u * lanes, lanes), lanes)
        return pltpu.make_async_copy(props_ref.at[0, :, at], block_ref.at[u], in_sems.at[u])

    def send(u):
        at = pl.ds(u * per, per)
        return pltpu.make_async_copy(held_ref.at[at], out_ref.at[at], out_sems.at[u])

    for u in range(ahead):
        fetch(u).start()

    def step(u, carry):
        fetch(u).wait()

        @pl.when(u + ahead < steps)
        def _():
            fetch(u + ahead).start()

        for k in range(per):
            t = u * per + k
            idx = idx_ref[t]
            rows = [idx[r : r + 1, :] for r in range(3)] + [doubled(idx[3:4, :], False)]
            picked = pick_sites(block_ref[u, :, k * sites : (k + 1) * sites], rows)
            for l in range(NSC):
                held_ref[t, :, l * MAIN : (l + 1) * MAIN] = ordered_rows(picked[:, 0:MAIN], l).astype(
                    jnp.bfloat16
                )
            for l in range(0, NSC, 2):
                at = NSC * MAIN + 64 * l
                held_ref[t, :, at : at + 128] = two_to_a_tile(picked[:, MAIN : MAIN + 128], l)
        send(u).start()
        return carry

    lax.fori_loop(0, steps, step, 0)
    for u in range(steps):
        send(u).wait()


def rest_gather_kernel(idx_ref, props_ref, out_ref):
    hot = one_hot_columns(doubled(idx_ref[0, 3:4, :], True), props_ref.shape[2])
    picked = jnp.dot(props_ref[0], hot, preferred_element_type=jnp.float32)
    for l in range(0, NSC, 2):
        out_ref[0, :, 64 * l : 64 * l + 128] = two_to_a_tile(picked, l)


def pair_pick_kernel(me_ref, idx_ref, props_ref, out_ref):
    slabs = idx_ref.shape[0]
    sites = props_ref.shape[2] // slabs
    lax.fori_loop(0, slabs, functools.partial(pick_block, me_ref, idx_ref, props_ref, out_ref, sites), 0)


def pick_block(me_ref, idx_ref, props_ref, out_ref, sites, t, carry):
    idx = idx_ref[t]
    far = 1 << 20
    ids = lax.broadcasted_iota(jnp.int32, (64, 128), 0)
    lane = lax.broadcasted_iota(jnp.int32, (1, 128), 1)
    first = jnp.full((64, 128), far, jnp.int32)
    last = jnp.full((64, 128), -1, jnp.int32)
    for r in range(4):
        combo = idx[8 + r : 9 + r, :]
        key = jnp.where(combo // 16 % 16 == me_ref[0], combo // 256 * 16 + combo % 16, -1)
        code = (r * 128 + lane) * sites + idx[4 + r : 5 + r, :]
        mine = ids == key
        first = jnp.minimum(first, jnp.where(mine, code, far))
        last = jnp.maximum(last, jnp.where(mine, code, -1))
    first = jnp.min(first, axis=1, keepdims=True)
    last = jnp.max(last, axis=1, keepdims=True)
    found = jnp.concatenate([first, last], axis=0)
    place = jnp.where((found >= 0) & (found < far), found % sites, -1)
    hot = jnp.where(
        lax.broadcasted_iota(jnp.int32, (128, sites), 1) == place, 1.0, 0.0
    ).astype(jnp.bfloat16)
    block = props_ref[0, :, pl.ds(pl.multiple_of(t * sites, sites), sites)]
    out_ref[:, pl.ds(pl.multiple_of(t * 128, 128), 128)] = lax.dot_general(
        block, hot, (((1,), (1,)), ((), ())), preferred_element_type=jnp.float32
    ).astype(jnp.bfloat16)
    return carry


def coded(sums):
    groups, rows, lanes = sums.shape
    lane = lax.broadcasted_iota(jnp.int32, (groups, lanes), 1)
    tail_row = lax.broadcasted_iota(jnp.int32, (groups, 16, lanes), 1)
    tail = jnp.zeros((groups, 16, lanes), jnp.int32)
    whole, corners = [], []
    for c in range(rows // 40):
        part = sums[:, 40 * c : 40 * c + 40, :]
        peak = jnp.max(jnp.abs(part), axis=1)
        for d in (4, 2, 1):
            other = jnp.where(
                lane % (2 * d) < d, pltpu.roll(peak, lanes - d, 1), pltpu.roll(peak, d, 1)
            )
            peak = jnp.maximum(peak, other)
        shift = 14.0 - jnp.floor(jnp.log2(jnp.maximum(peak, 2.0**-112)))
        value = jnp.floor(part * jnp.exp2(shift)[:, None, :] + 0.5)
        value = jnp.clip(value, -32767.0, 32767.0)
        whole.append(value[:, 0:32, :].astype(jnp.int32))
        corner = value[:, 32:40, :]
        if c % 2:
            corners.append((even + pltpu.roll(corner, 4, 2)).astype(jnp.int32))
        even = corner
        tail = jnp.where(tail_row == c, shift.astype(jnp.int32)[:, None, :], tail)
    return jnp.concatenate(whole + corners + [tail], axis=1).astype(jnp.int16)


def decoded_sum(coded_ref):
    total = None
    for g in range(coded_ref.shape[0]):
        value = coded_ref[g].astype(jnp.int32).astype(jnp.float32)
        rows, lanes = value.shape
        low = lax.broadcasted_iota(jnp.int32, (8, lanes), 1) % 8 < 4
        classes = (rows - 16) // 36
        parts = []
        for c in range(classes):
            scale = jnp.exp2(-value[rows - 16 + c : rows - 15 + c, :])
            at = 32 * classes + 8 * (c // 2)
            corner = value[at : at + 8, :]
            if c % 2:
                corner = pltpu.roll(corner, lanes - 4, 1)
            parts.append(value[32 * c : 32 * c + 32, :] * scale)
            parts.append(jnp.where(low, corner * scale, 0.0))
        term = jnp.concatenate(parts, axis=0)
        total = term if total is None else total + term
    return total


def combo_kernel(
    more_ref, x_ref, rest_ref, w_ref, after_a, after_b, after_c,
    out_ref, held_ref, rest_held, acc_ref, sums_ref, sems,
):
    sources, _, lanes = x_ref.shape
    classes = w_ref.shape[0]
    depth = held_ref.shape[3]
    rest_depth = rest_held.shape[2]
    n = sources * 8

    def piece(s):
        at = pl.ds(pl.multiple_of(s * depth, depth), depth)
        return pltpu.make_async_copy(x_ref.at[:, :, at], held_ref.at[s], sems.at[s])

    for s in range(lanes // depth):
        piece(s).start()

    def products(wide, weights):
        rows = jnp.concatenate(
            [wide[:, 8 * t : 8 * t + 8, :].reshape(n, wide.shape[2]) for t in range(3)], axis=0
        )
        right = rows.astype(jnp.bfloat16)
        scaled = [rows * weights[c : c + 1, :] for c in range(classes)]
        left = jnp.concatenate(
            [scaled[c][n * t : n * t + n, :] for t in range(3) for c in range(classes)], axis=0
        ).astype(jnp.bfloat16)
        return [
            lax.dot_general(
                left[t * classes * n : (t + 1) * classes * n],
                right[t * n : (t + 2) * n]
                if t < 2
                else jnp.concatenate([right[2 * n :], right[0:n]], axis=0),
                (((1,), (1,)), ((), ())),
                preferred_element_type=jnp.float32,
            )
            for t in range(3)
        ]

    def chunk(s, carry):
        piece(s).wait()
        at = pl.ds(pl.multiple_of(s * depth, depth), depth)
        parts = products(held_ref[s].astype(jnp.float32), w_ref[:, at])

        @pl.when(s == 0)
        def _():
            for t in range(3):
                acc_ref[t] = parts[t]

        @pl.when(s > 0)
        def _():
            for t in range(3):
                acc_ref[t] += parts[t]

        return carry

    lax.fori_loop(0, lanes // depth, chunk, 0)

    @pl.when(more_ref[0] > 0)
    def _():
        copy = pltpu.make_async_copy(rest_ref, rest_held, sems.at[lanes // depth])
        copy.start()
        copy.wait()
        parts = products(rest_held[...].astype(jnp.float32), w_ref[:, lanes : lanes + rest_depth])
        for t in range(3):
            acc_ref[t] += parts[t]

    low_row = lax.broadcasted_iota(jnp.int32, (n, n), 0) % 8 < 4
    low_lane = lax.broadcasted_iota(jnp.int32, (n, n), 1) % 8 < 4

    def swap_rows(m):
        return pltpu.roll(m.reshape(sources, 8, n), 4, 1).reshape(n, n)

    def swap_lanes(m):
        return jnp.where(low_lane, pltpu.roll(m, n - 4, 1), pltpu.roll(m, 4, 1))

    for c in range(classes):

        def blk(left_tile, right_tile):
            at = n * ((right_tile - left_tile) % 3)
            return acc_ref[left_tile, c * n : c * n + n, at : at + n]

        re = (blk(0, 0) + blk(1, 1)).T
        im = blk(0, 1).T - blk(0, 1)
        a, b = blk(2, 0).T, swap_lanes(blk(1, 2))
        wide_col = jnp.where(low_lane, a + b, b - a)
        a, b = blk(2, 0), swap_rows(blk(1, 2).T)
        tall_row = jnp.where(low_row, a + b, a - b)
        a = blk(2, 2)
        b = swap_lanes(swap_rows(a))
        corner = jnp.where(low_row, jnp.where(low_lane, a + b, a - b), 0.0).T
        for k, m in enumerate((re, im, wide_col, tall_row, corner)):
            at = (c * 5 + k) * 8
            sums_ref[:, at : at + 8, :] = m.reshape(sources, 8, n)
    out_ref[...] = coded(sums_ref[...])


def reduce_kernel(coded_ref, out_ref):
    total = coded(decoded_sum(coded_ref)[None])
    for g in range(out_ref.shape[0]):
        out_ref[g] = total[0]


def spread_matrix():
    out = np.zeros((5, 8, 8, 768), np.float32)

    def put(k, r, q, j, i, imag):
        at = j * NSC + i
        half = NSC * NSC
        if imag:
            out[k, r, q, half + at] = -1.0
            out[k, r, q, 384 + at] = 1.0
        else:
            out[k, r, q, at] = 1.0
            out[k, r, q, 384 + half + at] = 1.0

    for r in range(8):
        for q in range(8):
            put(0, r, q, r, q, False)
            put(1, r, q, r, q, True)
            put(2, r, q, r, 8 + q % 4, q >= 4)
            put(3, r, q, 8 + r % 4, q, r >= 4)
            if q < 4:
                put(4, r, q, 8 + r % 4, 8 + q, r >= 4)
    return out.reshape(320, 768)


def fold_matrix():
    r = np.arange(1024)[:, None] // 128
    q = np.arange(1024)[:, None] % 8
    return (np.arange(64)[None, :] == r * 8 + q).astype(np.float32)


def amplitude_kernel(sums_ref, fold_ref, spread_ref, partner_ref, out_ref):
    classes, sources = 4, 16
    combos = classes * sources
    sums = decoded_sum(sums_ref)
    own = (
        lax.broadcasted_iota(jnp.int32, (sources, 128), 1) // 8
        == lax.broadcasted_iota(jnp.int32, (sources, 128), 0)
    )
    total = jnp.zeros((2 * combos, 768), jnp.float32)
    for k in range(5):
        tall = []
        for c in range(classes):
            at = (c * 5 + k) * 8
            tall.append(
                jnp.concatenate(
                    [
                        jnp.where(own, jnp.broadcast_to(sums[at + r : at + r + 1, :], (sources, 128)), 0.0)
                        for r in range(8)
                    ],
                    axis=1,
                )
            )
        tall = jnp.concatenate(tall, axis=0)
        high = tall.astype(jnp.bfloat16)
        low = (tall - high.astype(jnp.float32)).astype(jnp.bfloat16)
        both = jnp.concatenate([high, low], axis=0)
        folded = jnp.dot(both, fold_ref[...], preferred_element_type=jnp.float32)
        total += jnp.dot(
            folded.astype(jnp.bfloat16),
            spread_ref[64 * k : 64 * k + 64, :],
            preferred_element_type=jnp.float32,
        )
    rows = partner_ref.shape[0]
    probe = jnp.concatenate([total[:, 0:rows], total[:, 384 : 384 + rows]], axis=0).astype(jnp.bfloat16)
    traces = jnp.dot(probe, partner_ref[...], preferred_element_type=jnp.float32)
    mine = (
        lax.broadcasted_iota(jnp.int32, (combos, 128), 1) % combos
        == lax.broadcasted_iota(jnp.int32, (combos, 128), 0)
    )
    for t in range(out_ref.shape[0]):
        lanes = slice(t * 128, t * 128 + 128)
        for part in range(2):
            at = part * 2 * combos
            value = traces[at : at + combos, lanes] + traces[at + combos : at + 2 * combos, lanes]
            out_ref[t, part : part + 1, :] = jnp.sum(jnp.where(mine, value, 0.0), axis=0, keepdims=True)


def home_kernel(back_ref, slot_ref, source_ref, out_ref):
    sources, _, slots = back_ref.shape
    pairs = slot_ref.shape[1]
    rest = jnp.concatenate([back_ref[:, 0, :], back_ref[:, 1, :]], axis=0)
    parts = []
    for _ in range(3):
        part = rest.astype(jnp.bfloat16)
        rest = rest - part.astype(jnp.float32)
        parts.append(part)
    hot = jnp.where(
        lax.broadcasted_iota(jnp.int32, (slots, pairs), 0) == slot_ref[...], 1.0, 0.0
    ).astype(jnp.bfloat16)
    spread = jnp.dot(jnp.concatenate(parts, axis=0), hot, preferred_element_type=jnp.float32)
    n = 2 * sources
    value = (spread[0:n] + spread[n : 2 * n]) + spread[2 * n : 3 * n]
    mine = lax.broadcasted_iota(jnp.int32, (sources, pairs), 0) == source_ref[...]
    for part in range(2):
        out_ref[part : part + 1, :] = jnp.sum(
            jnp.where(mine, value[part * sources : (part + 1) * sources], 0.0), axis=0, keepdims=True
        )


def params(mebibytes):
    return pltpu.CompilerParams(vmem_limit_bytes=mebibytes * 1024 * 1024)


IN_VMEM = pl.BlockSpec(memory_space=pltpu.VMEM)


def local(propagators, z_sites, z_class, kernel_table, pair_combo, pair_site):
    slabs = lax.axis_size("ta")
    blocks = lax.axis_size("sa")
    me = lax.axis_index("ta")
    rows = propagators.shape[1]
    site_count = propagators.shape[2] // slabs
    z_count = z_sites.shape[0]
    pair_count = pair_site.shape[0]
    classes = kernel_table.shape[0]
    depth = NSC * SENT
    rest_depth = NSC * (z_count - SENT)

    def exchange(array, axis):
        return lax.all_to_all(array, axis, split_axis=0, concat_axis=0, tiled=True)

    z_table = z_sites.reshape(-1, 128)
    lists = pl.pallas_call(
        list_kernel,
        in_specs=[pl.BlockSpec(memory_space=pl.ANY)] * 3,
        out_specs=IN_VMEM,
        out_shape=jax.ShapeDtypeStruct((slabs, 16, 128), jnp.int32),
        scratch_shapes=[pltpu.VMEM((z_count // 128, 128), jnp.int32)] * 3 + [pltpu.SemaphoreType.DMA((3,))],
        compiler_params=params(60),
        name="lists",
    )(z_table, pair_site.reshape(-1, 128), pair_combo.reshape(-1, 128))
    own_list = lists[0:1]
    lists = exchange(lists, "ta")
    more = jnp.any(lists[:, 12, 0] > SENT)

    one_hot = (
        z_class[None, :] == jnp.arange(kernel_table.shape[1], dtype=jnp.int32)[:, None]
    ).astype(jnp.float32)
    weights = jnp.dot(kernel_table, one_hot, precision=lax.Precision.HIGHEST)

    steps = slabs // 4
    z_rows = pl.pallas_call(
        z_gather_kernel,
        in_specs=[IN_VMEM, pl.BlockSpec(memory_space=pl.ANY), pl.BlockSpec(memory_space=pl.ANY)],
        out_specs=pl.BlockSpec(memory_space=pl.ANY),
        out_shape=jax.ShapeDtypeStruct((slabs, 24, depth), jnp.bfloat16),
        scratch_shapes=[
            pltpu.VMEM((steps, rows, slabs // steps * site_count), jnp.bfloat16),
            pltpu.VMEM((slabs, 24, depth), jnp.bfloat16),
            pltpu.SemaphoreType.DMA((steps,)),
            pltpu.SemaphoreType.DMA((steps,)),
        ],
        compiler_params=params(50),
        cost_estimate=pl.CostEstimate(
            flops=2 * rows * site_count * z_count * slabs, bytes_accessed=15_000_000, transcendentals=0
        ),
        name="z_gather",
    )(lists, propagators, weights)
    z_rows = exchange(z_rows, "ta")

    def send_rest(lists, propagators, blank):
        rest = pl.pallas_call(
            rest_gather_kernel,
            grid=(slabs,),
            in_specs=[
                pl.BlockSpec((1,) + lists.shape[1:], lambda t: (t, 0, 0)),
                pl.BlockSpec((1, rows, site_count), lambda t: (0, 0, t)),
            ],
            out_specs=pl.BlockSpec((1, 24, rest_depth), lambda t: (t, 0, 0)),
            out_shape=jax.ShapeDtypeStruct((slabs, 24, rest_depth), jnp.bfloat16),
            compiler_params=params(24),
            name="rest_gather",
        )(lists, propagators)
        return exchange(rest, "ta")

    def no_rest(lists, propagators, blank):
        return blank

    blank = jnp.zeros((slabs, 24, rest_depth), jnp.bfloat16)
    after, blank, z_rows = lax.optimization_barrier((more, blank, z_rows))
    rest_rows = lax.cond(after, send_rest, no_rest, lists, propagators, blank)
    added = pl.pallas_call(
        weight_kernel,
        in_specs=[IN_VMEM] * 3,
        out_specs=IN_VMEM,
        out_shape=jax.ShapeDtypeStruct((classes, depth + rest_depth), jnp.float32),
        compiler_params=params(16),
        name="weights",
    )(weights, z_table, own_list)

    slots = 128
    partner = pl.pallas_call(
        pair_pick_kernel,
        in_specs=[pl.BlockSpec(memory_space=pltpu.SMEM), IN_VMEM, IN_VMEM],
        out_specs=IN_VMEM,
        out_shape=jax.ShapeDtypeStruct((rows, slabs * slots), jnp.bfloat16),
        compiler_params=params(16),
        cost_estimate=pl.CostEstimate(
            flops=2 * rows * site_count * slots * slabs, bytes_accessed=11_000_000, transcendentals=0
        ),
        name="pair_pick",
    )(me.astype(jnp.int32).reshape(1), lists, propagators)

    combo_ids = pair_combo[:, 0]
    counter = jnp.arange(pair_count, dtype=jnp.int32)
    second = jnp.any(
        (combo_ids[:, None] == combo_ids[None, :]) & (counter[None, :] < counter[:, None]), axis=1
    )
    slot = combo_ids // 256 * 16 + combo_ids % 16 + jnp.where(second, 64, 0)
    slot = slot.reshape(1, -1)
    source = (combo_ids // 16 % 16).reshape(1, -1)

    sums = pl.pallas_call(
        combo_kernel,
        in_specs=[
            pl.BlockSpec(memory_space=pltpu.SMEM),
            pl.BlockSpec(memory_space=pl.ANY),
            pl.BlockSpec(memory_space=pl.ANY),
            IN_VMEM,
        ]
        + [pl.BlockSpec(memory_space=pl.ANY)] * 3,
        out_specs=IN_VMEM,
        out_shape=jax.ShapeDtypeStruct((slabs, classes * 36 + 16, 128), jnp.int16),
        scratch_shapes=[
            pltpu.VMEM((3, slabs, 24, depth // 3), jnp.bfloat16),
            pltpu.VMEM((slabs, 24, rest_depth), jnp.bfloat16),
            pltpu.VMEM((3, classes * slabs * 8, slabs * 16), jnp.float32),
            pltpu.VMEM((slabs, classes * 40, 128), jnp.float32),
            pltpu.SemaphoreType.DMA((4,)),
        ],
        compiler_params=params(32),
        cost_estimate=pl.CostEstimate(
            flops=2 * classes * 384 * 384 * depth, bytes_accessed=6_000_000, transcendentals=0
        ),
        name="combo_sums",
    )(more.astype(jnp.int32).reshape(1), z_rows, rest_rows, added, partner, slot, source)

    sums = pl.pallas_call(
        reduce_kernel,
        in_specs=[IN_VMEM],
        out_specs=IN_VMEM,
        out_shape=jax.ShapeDtypeStruct((blocks,) + sums.shape[1:], jnp.int16),
        compiler_params=params(16),
        name="reduce_sums",
    )(exchange(sums, "ta"))
    sums = exchange(sums, "sa")

    found = pl.pallas_call(
        amplitude_kernel,
        in_specs=[IN_VMEM] * 4,
        out_specs=IN_VMEM,
        out_shape=jax.ShapeDtypeStruct((slabs, 2, slots), jnp.float32),
        compiler_params=params(32),
        name="amplitudes",
    )(
        sums,
        jnp.asarray(fold_matrix(), jnp.bfloat16),
        jnp.asarray(spread_matrix(), jnp.bfloat16),
        partner,
    )
    back = exchange(found, "ta")
    return pl.pallas_call(
        home_kernel,
        in_specs=[IN_VMEM] * 3,
        out_specs=IN_VMEM,
        out_shape=jax.ShapeDtypeStruct((2, pair_count), jnp.float32),
        compiler_params=params(16),
        name="home",
    )(back, slot, source)


def solution(mesh):
    placed = (
        P("ta", None, "sa"),
        P(("ta", "sa")),
        P(("ta", "sa")),
        P(),
        P(("ta", "sa"), None),
        P(("ta", "sa")),
    )
    return jax.shard_map(
        local, mesh=mesh, in_specs=placed, out_specs=P(None, ("ta", "sa")), check_vma=False
    )
```

```python
import functools

import jax
import jax.numpy as jnp
import numpy as np
from jax import lax
from jax.experimental import pallas as pl
from jax.experimental.pallas import tpu as pltpu
from jax.sharding import PartitionSpec as P

NSC = 12
MAIN = 384
SENT = 448

def one_hot_columns(idx_row, count):
    rows = lax.broadcasted_iota(jnp.int32, (count, idx_row.shape[1]), 0)
    return jnp.where(rows == idx_row, 1.0, 0.0).astype(jnp.bfloat16)


def doubled(row, upper):
    other = pltpu.roll(row, 64, 1)
    low = lax.broadcasted_iota(jnp.int32, row.shape, 1) < 64
    return jnp.where(low, other, row) if upper else jnp.where(low, row, other)


def as_column(row):
    eye = lax.broadcasted_iota(jnp.int32, (128, 128), 0) == lax.broadcasted_iota(jnp.int32, (128, 128), 1)
    return jnp.sum(jnp.where(eye, row, 0.0), axis=1, keepdims=True)


def list_kernel(z_hbm, site_hbm, combo_hbm, out_ref, z_ref, site_ref, combo_ref, sems):
    copies = [
        pltpu.make_async_copy(source, held, sems.at[k])
        for k, (source, held) in enumerate(((z_hbm, z_ref), (site_hbm, site_ref), (combo_hbm, combo_ref)))
    ]
    for copy in copies:
        copy.start()
    for copy in copies:
        copy.wait()
    groups = z_ref.shape[0]
    row = [z_ref[g : g + 1, :].astype(jnp.float32) for g in range(groups)]
    col = [as_column(r) for r in row]
    sub = lax.broadcasted_iota(jnp.int32, (128, 128), 0)
    lane = lax.broadcasted_iota(jnp.int32, (128, 128), 1)
    first_col, first_row = [], []
    for g in range(groups):
        again_col = jnp.where((col[g] == row[g]) & (lane < sub), 1.0, 0.0)
        again_row = jnp.where((col[g] == row[g]) & (sub < lane), 1.0, 0.0)
        for h in range(g):
            again_col = jnp.maximum(again_col, jnp.where(col[g] == row[h], 1.0, 0.0))
            again_row = jnp.maximum(again_row, jnp.where(col[h] == row[g], 1.0, 0.0))
        first_col.append(1.0 - jnp.max(again_col, axis=1, keepdims=True))
        first_row.append(1.0 - jnp.max(again_row, axis=0, keepdims=True))
    count = jnp.zeros((1, 1), jnp.float32)
    place = []
    for g in range(groups):
        here = jnp.sum(jnp.where(lane < sub, first_row[g], 0.0), axis=1, keepdims=True) + count
        place.append(jnp.where(first_col[g] > 0.5, here, -1.0))
        count = count + jnp.sum(first_row[g], axis=1, keepdims=True)
    block = []
    for g in range(groups):
        want = (lane + 128 * g).astype(jnp.float32)
        total = jnp.zeros((128, 128), jnp.float32)
        for h in range(groups):
            total += jnp.where(place[h] == want, col[h], 0.0)
        found = jnp.sum(total, axis=0, keepdims=True)
        block.append(jnp.where(want[0:1, :] < count, found, -1.0).astype(jnp.int32))
    block += [site_ref[...], combo_ref[...]]
    block.append(jnp.broadcast_to(count, (16 - 3 * groups, 128)).astype(jnp.int32))
    block = jnp.concatenate(block, axis=0)
    for t in range(out_ref.shape[0]):
        out_ref[t] = block


def weight_kernel(w_ref, z_ref, idx_ref, out_ref):
    classes = w_ref.shape[0]
    groups = z_ref.shape[0]
    hot = []
    for g in range(groups):
        col = as_column(z_ref[g : g + 1, :].astype(jnp.float32))
        hot.append(
            jnp.concatenate(
                [
                    jnp.where(col == idx_ref[0, h : h + 1, :].astype(jnp.float32), 1.0, 0.0)
                    for h in range(groups)
                ],
                axis=1,
            )
        )
    hot = jnp.concatenate(hot, axis=0).astype(jnp.bfloat16)
    rest = w_ref[...]
    added = jnp.zeros(rest.shape, jnp.float32)
    for _ in range(3):
        part = rest.astype(jnp.bfloat16)
        rest = rest - part.astype(jnp.float32)
        added += jnp.dot(part, hot, preferred_element_type=jnp.float32)
    edge = added[:, MAIN : MAIN + 128]
    for l in range(NSC):
        out_ref[:, l * MAIN : (l + 1) * MAIN] = added[:, 0:MAIN]
    for k, upper in ((0, False), (1, True)):
        for m in range(NSC // 2):
            at = NSC * (MAIN + 64 * k) + 128 * m
            out_ref[:, at : at + 128] = doubled(edge, upper)


def ordered_rows(picked, l):
    re, im = l * NSC, NSC * NSC + l * NSC
    return jnp.concatenate(
        [picked[re : re + 8], picked[im : im + 8], picked[re + 8 : re + 12], picked[im + 8 : im + 12]],
        axis=0,
    )


def two_to_a_tile(picked, l):
    low = lax.broadcasted_iota(jnp.int32, (24, 128), 1) < 64
    return jnp.where(low, ordered_rows(picked, l), ordered_rows(picked, l + 1)).astype(jnp.bfloat16)


def pick_sites(block, rows):
    count, half = block.shape[0], block.shape[1] // 2
    hot = jnp.concatenate([one_hot_columns(r % half, half) for r in rows], axis=1)
    upper = jnp.concatenate(rows, axis=1) >= half
    both = jnp.concatenate([block[:, 0:half], block[:, half:]], axis=0)
    picked = jnp.dot(both, hot, preferred_element_type=jnp.float32)
    return jnp.where(upper, picked[count:], picked[0:count])


def z_gather_kernel(idx_ref, props_ref, after_ref, out_ref, block_ref, held_ref, in_sems, out_sems):
    slabs = out_ref.shape[0]
    sites = props_ref.shape[2] // slabs
    small, first, big = 2, 4, 4
    stages = ((0, small, first // small), (first, big, (slabs - first) // big))

    def fetch(at, number):
        lanes = pl.ds(pl.multiple_of(at * sites, sites), number * sites)
        return pltpu.make_async_copy(
            props_ref.at[0, :, lanes], block_ref.at[:, lanes], in_sems.at[at]
        )

    def send(at, number):
        part = pl.ds(at, number)
        return pltpu.make_async_copy(held_ref.at[part], out_ref.at[part], out_sems.at[at])

    for start, per, steps in stages:
        for u in range(steps):
            fetch(start + u * per, per).start()

    for start, per, steps in stages:

        def step(u, carry):
            at = start + u * per
            fetch(at, per).wait()
            for k in range(per):
                t = at + k
                idx = idx_ref[t]
                rows = [idx[r : r + 1, :] for r in range(3)] + [doubled(idx[3:4, :], False)]
                lanes = pl.ds(pl.multiple_of(t * sites, sites), sites)
                picked = pick_sites(block_ref[:, lanes], rows)
                for l in range(NSC):
                    held_ref[t, :, l * MAIN : (l + 1) * MAIN] = ordered_rows(
                        picked[:, 0:MAIN], l
                    ).astype(jnp.bfloat16)
                for l in range(0, NSC, 2):
                    to = NSC * MAIN + 64 * l
                    held_ref[t, :, to : to + 128] = two_to_a_tile(picked[:, MAIN : MAIN + 128], l)
            send(at, per).start()
            return carry

        lax.fori_loop(0, steps, step, 0)

    for start, per, steps in stages:
        for u in range(steps):
            send(start + u * per, per).wait()


def rest_gather_kernel(idx_ref, props_ref, out_ref):
    hot = one_hot_columns(doubled(idx_ref[0, 3:4, :], True), props_ref.shape[2])
    picked = jnp.dot(props_ref[0], hot, preferred_element_type=jnp.float32)
    for l in range(0, NSC, 2):
        out_ref[0, :, 64 * l : 64 * l + 128] = two_to_a_tile(picked, l)


def pair_pick_kernel(me_ref, idx_ref, props_ref, out_ref):
    slabs = idx_ref.shape[0]
    sites = props_ref.shape[2] // slabs
    lax.fori_loop(0, slabs, functools.partial(pick_block, me_ref, idx_ref, props_ref, out_ref, sites), 0)


def pick_block(me_ref, idx_ref, props_ref, out_ref, sites, t, carry):
    idx = idx_ref[t]
    far = 1 << 20
    ids = lax.broadcasted_iota(jnp.int32, (64, 128), 0)
    lane = lax.broadcasted_iota(jnp.int32, (1, 128), 1)
    first = jnp.full((64, 128), far, jnp.int32)
    last = jnp.full((64, 128), -1, jnp.int32)
    for r in range(4):
        combo = idx[8 + r : 9 + r, :]
        key = jnp.where(combo // 16 % 16 == me_ref[0], combo // 256 * 16 + combo % 16, -1)
        code = (r * 128 + lane) * sites + idx[4 + r : 5 + r, :]
        mine = ids == key
        first = jnp.minimum(first, jnp.where(mine, code, far))
        last = jnp.maximum(last, jnp.where(mine, code, -1))
    first = jnp.min(first, axis=1, keepdims=True)
    last = jnp.max(last, axis=1, keepdims=True)
    found = jnp.concatenate([first, last], axis=0)
    place = jnp.where((found >= 0) & (found < far), found % sites, -1)
    hot = jnp.where(
        lax.broadcasted_iota(jnp.int32, (128, sites), 1) == place, 1.0, 0.0
    ).astype(jnp.bfloat16)
    block = props_ref[0, :, pl.ds(pl.multiple_of(t * sites, sites), sites)]
    out_ref[:, pl.ds(pl.multiple_of(t * 128, 128), 128)] = lax.dot_general(
        block, hot, (((1,), (1,)), ((), ())), preferred_element_type=jnp.float32
    ).astype(jnp.bfloat16)
    return carry


def coded(sums):
    groups, rows, lanes = sums.shape
    lane = lax.broadcasted_iota(jnp.int32, (groups, lanes), 1)
    tail_row = lax.broadcasted_iota(jnp.int32, (groups, 8, lanes), 1)
    tail = jnp.zeros((groups, 8, lanes), jnp.int32)
    whole, corners = [], []
    for c in range(rows // 40):
        part = sums[:, 40 * c : 40 * c + 40, :]
        peak = jnp.max(jnp.abs(part), axis=1)
        for d in (4, 2, 1):
            other = jnp.where(
                lane % (2 * d) < d, pltpu.roll(peak, lanes - d, 1), pltpu.roll(peak, d, 1)
            )
            peak = jnp.maximum(peak, other)
        shift = 14.0 - jnp.floor(jnp.log2(jnp.maximum(peak, 2.0**-112)))
        value = jnp.floor(part * jnp.exp2(shift)[:, None, :] + 0.5)
        value = jnp.clip(value, -32767.0, 32767.0)
        whole.append(value[:, 0:32, :].astype(jnp.int32))
        corner = value[:, 32:40, :]
        if c % 2:
            corners.append((even + pltpu.roll(corner, 4, 2)).astype(jnp.int32))
        even = corner
        tail = jnp.where(tail_row == c, shift.astype(jnp.int32)[:, None, :], tail)
    return jnp.concatenate(whole + corners + [tail], axis=1).astype(jnp.int16)


def decoded_sum(coded_ref):
    total = None
    for g in range(coded_ref.shape[0]):
        value = coded_ref[g].astype(jnp.int32).astype(jnp.float32)
        rows, lanes = value.shape
        low = lax.broadcasted_iota(jnp.int32, (8, lanes), 1) % 8 < 4
        classes = (rows - 8) // 36
        parts = []
        for c in range(classes):
            scale = jnp.exp2(-value[rows - 8 + c : rows - 7 + c, :])
            at = 32 * classes + 8 * (c // 2)
            corner = value[at : at + 8, :]
            if c % 2:
                corner = pltpu.roll(corner, lanes - 4, 1)
            parts.append(value[32 * c : 32 * c + 32, :] * scale)
            parts.append(jnp.where(low, corner * scale, 0.0))
        term = jnp.concatenate(parts, axis=0)
        total = term if total is None else total + term
    return total


def combo_kernel(
    more_ref, x_ref, rest_ref, w_ref, after_a, after_b, after_c,
    out_ref, held_ref, rest_held, acc_ref, sums_ref, sems,
):
    sources, _, lanes = x_ref.shape
    classes = w_ref.shape[0]
    depth = held_ref.shape[3]
    rest_depth = rest_held.shape[2]
    n = sources * 8

    def piece(s):
        at = pl.ds(pl.multiple_of(s * depth, depth), depth)
        return pltpu.make_async_copy(x_ref.at[:, :, at], held_ref.at[s], sems.at[s])

    for s in range(lanes // depth):
        piece(s).start()

    def products(wide, weights):
        rows = jnp.concatenate(
            [wide[:, 8 * t : 8 * t + 8, :].reshape(n, wide.shape[2]) for t in range(3)], axis=0
        )
        right = rows.astype(jnp.bfloat16)
        scaled = [rows * weights[c : c + 1, :] for c in range(classes)]
        left = jnp.concatenate(
            [scaled[c][n * t : n * t + n, :] for t in range(3) for c in range(classes)], axis=0
        ).astype(jnp.bfloat16)
        return [
            lax.dot_general(
                left[t * classes * n : (t + 1) * classes * n],
                right[t * n : (t + 2) * n]
                if t < 2
                else jnp.concatenate([right[2 * n :], right[0:n]], axis=0),
                (((1,), (1,)), ((), ())),
                preferred_element_type=jnp.float32,
            )
            for t in range(3)
        ]

    def chunk(s, carry):
        piece(s).wait()
        at = pl.ds(pl.multiple_of(s * depth, depth), depth)
        parts = products(held_ref[s].astype(jnp.float32), w_ref[:, at])

        @pl.when(s == 0)
        def _():
            for t in range(3):
                acc_ref[t] = parts[t]

        @pl.when(s > 0)
        def _():
            for t in range(3):
                acc_ref[t] += parts[t]

        return carry

    lax.fori_loop(0, lanes // depth, chunk, 0)

    @pl.when(more_ref[0] > 0)
    def _():
        copy = pltpu.make_async_copy(rest_ref, rest_held, sems.at[lanes // depth])
        copy.start()
        copy.wait()
        parts = products(rest_held[...].astype(jnp.float32), w_ref[:, lanes : lanes + rest_depth])
        for t in range(3):
            acc_ref[t] += parts[t]

    low_row = lax.broadcasted_iota(jnp.int32, (n, n), 0) % 8 < 4
    low_lane = lax.broadcasted_iota(jnp.int32, (n, n), 1) % 8 < 4

    def swap_rows(m):
        return pltpu.roll(m.reshape(sources, 8, n), 4, 1).reshape(n, n)

    def swap_lanes(m):
        return jnp.where(low_lane, pltpu.roll(m, n - 4, 1), pltpu.roll(m, 4, 1))

    for c in range(classes):

        def blk(left_tile, right_tile):
            at = n * ((right_tile - left_tile) % 3)
            return acc_ref[left_tile, c * n : c * n + n, at : at + n]

        re = (blk(0, 0) + blk(1, 1)).T
        im = blk(0, 1).T - blk(0, 1)
        a, b = blk(2, 0).T, swap_lanes(blk(1, 2))
        wide_col = jnp.where(low_lane, a + b, b - a)
        a, b = blk(2, 0), swap_rows(blk(1, 2).T)
        tall_row = jnp.where(low_row, a + b, a - b)
        a = blk(2, 2)
        b = swap_lanes(swap_rows(a))
        corner = jnp.where(low_row, jnp.where(low_lane, a + b, a - b), 0.0).T
        for k, m in enumerate((re, im, wide_col, tall_row, corner)):
            at = (c * 5 + k) * 8
            sums_ref[:, at : at + 8, :] = m.reshape(sources, 8, n)
    out_ref[...] = coded(sums_ref[...])


def reduce_kernel(coded_ref, out_ref):
    total = coded(decoded_sum(coded_ref)[None])
    for g in range(out_ref.shape[0]):
        out_ref[g] = total[0]


def spread_matrix():
    out = np.zeros((5, 8, 8, 768), np.float32)

    def put(k, r, q, j, i, imag):
        at = j * NSC + i
        half = NSC * NSC
        if imag:
            out[k, r, q, half + at] = -1.0
            out[k, r, q, 384 + at] = 1.0
        else:
            out[k, r, q, at] = 1.0
            out[k, r, q, 384 + half + at] = 1.0

    for r in range(8):
        for q in range(8):
            put(0, r, q, r, q, False)
            put(1, r, q, r, q, True)
            put(2, r, q, r, 8 + q % 4, q >= 4)
            put(3, r, q, 8 + r % 4, q, r >= 4)
            if q < 4:
                put(4, r, q, 8 + r % 4, 8 + q, r >= 4)
    return out.reshape(320, 768)


def fold_matrix():
    r = np.arange(1024)[:, None] // 128
    q = np.arange(1024)[:, None] % 8
    return (np.arange(64)[None, :] == r * 8 + q).astype(np.float32)


def amplitude_kernel(sums_ref, fold_ref, spread_ref, partner_ref, out_ref):
    classes, sources = 4, 16
    combos = classes * sources
    sums = decoded_sum(sums_ref)
    own = (
        lax.broadcasted_iota(jnp.int32, (sources, 128), 1) // 8
        == lax.broadcasted_iota(jnp.int32, (sources, 128), 0)
    )
    total = jnp.zeros((2 * combos, 768), jnp.float32)
    for k in range(5):
        tall = []
        for c in range(classes):
            at = (c * 5 + k) * 8
            tall.append(
                jnp.concatenate(
                    [
                        jnp.where(own, jnp.broadcast_to(sums[at + r : at + r + 1, :], (sources, 128)), 0.0)
                        for r in range(8)
                    ],
                    axis=1,
                )
            )
        tall = jnp.concatenate(tall, axis=0)
        high = tall.astype(jnp.bfloat16)
        low = (tall - high.astype(jnp.float32)).astype(jnp.bfloat16)
        both = jnp.concatenate([high, low], axis=0)
        folded = jnp.dot(both, fold_ref[...], preferred_element_type=jnp.float32)
        total += jnp.dot(
            folded.astype(jnp.bfloat16),
            spread_ref[64 * k : 64 * k + 64, :],
            preferred_element_type=jnp.float32,
        )
    rows = partner_ref.shape[0]
    probe = jnp.concatenate([total[:, 0:rows], total[:, 384 : 384 + rows]], axis=0).astype(jnp.bfloat16)
    traces = jnp.dot(probe, partner_ref[...], preferred_element_type=jnp.float32)
    mine = (
        lax.broadcasted_iota(jnp.int32, (combos, 128), 1) % combos
        == lax.broadcasted_iota(jnp.int32, (combos, 128), 0)
    )
    for t in range(out_ref.shape[0]):
        lanes = slice(t * 128, t * 128 + 128)
        for part in range(2):
            at = part * 2 * combos
            value = traces[at : at + combos, lanes] + traces[at + combos : at + 2 * combos, lanes]
            out_ref[t, part : part + 1, :] = jnp.sum(jnp.where(mine, value, 0.0), axis=0, keepdims=True)


def home_kernel(back_ref, slot_ref, source_ref, out_ref):
    sources, _, slots = back_ref.shape
    pairs = slot_ref.shape[1]
    rest = jnp.concatenate([back_ref[:, 0, :], back_ref[:, 1, :]], axis=0)
    parts = []
    for _ in range(3):
        part = rest.astype(jnp.bfloat16)
        rest = rest - part.astype(jnp.float32)
        parts.append(part)
    hot = jnp.where(
        lax.broadcasted_iota(jnp.int32, (slots, pairs), 0) == slot_ref[...], 1.0, 0.0
    ).astype(jnp.bfloat16)
    spread = jnp.dot(jnp.concatenate(parts, axis=0), hot, preferred_element_type=jnp.float32)
    n = 2 * sources
    value = (spread[0:n] + spread[n : 2 * n]) + spread[2 * n : 3 * n]
    mine = lax.broadcasted_iota(jnp.int32, (sources, pairs), 0) == source_ref[...]
    for part in range(2):
        out_ref[part : part + 1, :] = jnp.sum(
            jnp.where(mine, value[part * sources : (part + 1) * sources], 0.0), axis=0, keepdims=True
        )


def params(mebibytes):
    return pltpu.CompilerParams(vmem_limit_bytes=mebibytes * 1024 * 1024)


IN_VMEM = pl.BlockSpec(memory_space=pltpu.VMEM)


def local(propagators, z_sites, z_class, kernel_table, pair_combo, pair_site):
    slabs = lax.axis_size("ta")
    blocks = lax.axis_size("sa")
    me = lax.axis_index("ta")
    rows = propagators.shape[1]
    site_count = propagators.shape[2] // slabs
    z_count = z_sites.shape[0]
    pair_count = pair_site.shape[0]
    classes = kernel_table.shape[0]
    depth = NSC * SENT
    rest_depth = NSC * (z_count - SENT)

    def exchange(array, axis):
        return lax.all_to_all(array, axis, split_axis=0, concat_axis=0, tiled=True)

    z_table = z_sites.reshape(-1, 128)
    lists = pl.pallas_call(
        list_kernel,
        in_specs=[pl.BlockSpec(memory_space=pl.ANY)] * 3,
        out_specs=IN_VMEM,
        out_shape=jax.ShapeDtypeStruct((slabs, 16, 128), jnp.int32),
        scratch_shapes=[pltpu.VMEM((z_count // 128, 128), jnp.int32)] * 3 + [pltpu.SemaphoreType.DMA((3,))],
        compiler_params=params(60),
        name="lists",
    )(z_table, pair_site.reshape(-1, 128), pair_combo.reshape(-1, 128))
    own_list = lists[0:1]
    lists = exchange(lists, "ta")
    more = jnp.any(lists[:, 12, 0] > SENT)

    one_hot = (
        z_class[None, :] == jnp.arange(kernel_table.shape[1], dtype=jnp.int32)[:, None]
    ).astype(jnp.float32)
    weights = jnp.dot(kernel_table, one_hot, precision=lax.Precision.HIGHEST)

    z_rows = pl.pallas_call(
        z_gather_kernel,
        in_specs=[IN_VMEM, pl.BlockSpec(memory_space=pl.ANY), pl.BlockSpec(memory_space=pl.ANY)],
        out_specs=pl.BlockSpec(memory_space=pl.ANY),
        out_shape=jax.ShapeDtypeStruct((slabs, 24, depth), jnp.bfloat16),
        scratch_shapes=[
            pltpu.VMEM((rows, slabs * site_count), jnp.bfloat16),
            pltpu.VMEM((slabs, 24, depth), jnp.bfloat16),
            pltpu.SemaphoreType.DMA((slabs,)),
            pltpu.SemaphoreType.DMA((slabs,)),
        ],
        compiler_params=params(50),
        cost_estimate=pl.CostEstimate(
            flops=2 * rows * site_count * z_count * slabs, bytes_accessed=15_000_000, transcendentals=0
        ),
        name="z_gather",
    )(lists, propagators, weights)
    z_rows = exchange(z_rows, "ta")

    def send_rest(lists, propagators, blank):
        rest = pl.pallas_call(
            rest_gather_kernel,
            grid=(slabs,),
            in_specs=[
                pl.BlockSpec((1,) + lists.shape[1:], lambda t: (t, 0, 0)),
                pl.BlockSpec((1, rows, site_count), lambda t: (0, 0, t)),
            ],
            out_specs=pl.BlockSpec((1, 24, rest_depth), lambda t: (t, 0, 0)),
            out_shape=jax.ShapeDtypeStruct((slabs, 24, rest_depth), jnp.bfloat16),
            compiler_params=params(24),
            name="rest_gather",
        )(lists, propagators)
        return exchange(rest, "ta")

    def no_rest(lists, propagators, blank):
        return blank

    blank = jnp.zeros((slabs, 24, rest_depth), jnp.bfloat16)
    after, blank, z_rows = lax.optimization_barrier((more, blank, z_rows))
    rest_rows = lax.cond(after, send_rest, no_rest, lists, propagators, blank)
    added = pl.pallas_call(
        weight_kernel,
        in_specs=[IN_VMEM] * 3,
        out_specs=IN_VMEM,
        out_shape=jax.ShapeDtypeStruct((classes, depth + rest_depth), jnp.float32),
        compiler_params=params(16),
        name="weights",
    )(weights, z_table, own_list)

    slots = 128
    partner = pl.pallas_call(
        pair_pick_kernel,
        in_specs=[pl.BlockSpec(memory_space=pltpu.SMEM), IN_VMEM, IN_VMEM],
        out_specs=IN_VMEM,
        out_shape=jax.ShapeDtypeStruct((rows, slabs * slots), jnp.bfloat16),
        compiler_params=params(16),
        cost_estimate=pl.CostEstimate(
            flops=2 * rows * site_count * slots * slabs, bytes_accessed=11_000_000, transcendentals=0
        ),
        name="pair_pick",
    )(me.astype(jnp.int32).reshape(1), lists, propagators)

    combo_ids = pair_combo[:, 0]
    counter = jnp.arange(pair_count, dtype=jnp.int32)
    second = jnp.any(
        (combo_ids[:, None] == combo_ids[None, :]) & (counter[None, :] < counter[:, None]), axis=1
    )
    slot = combo_ids // 256 * 16 + combo_ids % 16 + jnp.where(second, 64, 0)
    slot = slot.reshape(1, -1)
    source = (combo_ids // 16 % 16).reshape(1, -1)

    sums = pl.pallas_call(
        combo_kernel,
        in_specs=[
            pl.BlockSpec(memory_space=pltpu.SMEM),
            pl.BlockSpec(memory_space=pl.ANY),
            pl.BlockSpec(memory_space=pl.ANY),
            IN_VMEM,
        ]
        + [pl.BlockSpec(memory_space=pl.ANY)] * 3,
        out_specs=IN_VMEM,
        out_shape=jax.ShapeDtypeStruct((slabs, classes * 36 + 8, 128), jnp.int16),
        scratch_shapes=[
            pltpu.VMEM((3, slabs, 24, depth // 3), jnp.bfloat16),
            pltpu.VMEM((slabs, 24, rest_depth), jnp.bfloat16),
            pltpu.VMEM((3, classes * slabs * 8, slabs * 16), jnp.float32),
            pltpu.VMEM((slabs, classes * 40, 128), jnp.float32),
            pltpu.SemaphoreType.DMA((4,)),
        ],
        compiler_params=params(32),
        cost_estimate=pl.CostEstimate(
            flops=2 * classes * 384 * 384 * depth, bytes_accessed=6_000_000, transcendentals=0
        ),
        name="combo_sums",
    )(more.astype(jnp.int32).reshape(1), z_rows, rest_rows, added, partner, slot, source)

    sums = pl.pallas_call(
        reduce_kernel,
        in_specs=[IN_VMEM],
        out_specs=IN_VMEM,
        out_shape=jax.ShapeDtypeStruct((blocks,) + sums.shape[1:], jnp.int16),
        compiler_params=params(16),
        name="reduce_sums",
    )(exchange(sums, "ta"))
    sums = exchange(sums, "sa")

    found = pl.pallas_call(
        amplitude_kernel,
        in_specs=[IN_VMEM] * 4,
        out_specs=IN_VMEM,
        out_shape=jax.ShapeDtypeStruct((slabs, 2, slots), jnp.float32),
        compiler_params=params(32),
        name="amplitudes",
    )(
        sums,
        jnp.asarray(fold_matrix(), jnp.bfloat16),
        jnp.asarray(spread_matrix(), jnp.bfloat16),
        partner,
    )
    back = exchange(found, "ta")
    return pl.pallas_call(
        home_kernel,
        in_specs=[IN_VMEM] * 3,
        out_specs=IN_VMEM,
        out_shape=jax.ShapeDtypeStruct((2, pair_count), jnp.float32),
        compiler_params=params(16),
        name="home",
    )(back, slot, source)


def solution(mesh):
    placed = (
        P("ta", None, "sa"),
        P(("ta", "sa")),
        P(("ta", "sa")),
        P(),
        P(("ta", "sa"), None),
        P(("ta", "sa")),
    )
    return jax.shard_map(
        local, mesh=mesh, in_specs=placed, out_specs=P(None, ("ta", "sa")), check_vma=False
    )
```
